128 devices in a mesh: azim: 16 (over x_hi, z, core), axial: 8 (over y, x_lo).
Axes of the slice: x: 4 (x_hi: 2, x_lo: 2; x = x_hi * 2 + x_lo), y: 4, z: 4, core: 2. Of those that a mesh axis runs over, the one named last changes fastest.
Arguments:
- flow_state: float32 [11, 4, 4, 4, 16, 64, 128], P(None, None, None, None, 'azim', 'axial'), may hold values from -6 to 6
- velocity: float32 [3, 4, 4, 4, 16, 64, 128], P(None, None, None, None, 'azim', 'axial'), may hold values from -3 to 3
- inlet_state: float32 [11, 4, 4, 16, 128], P(None, None, None, 'azim'), may hold values from -6 to 6
- radial_inflow: float32 [2, 11, 4, 4, 16, 64], P(None, None, None, None, 'azim', 'axial'), may hold values from -6 to 6
- face_tags: int32 [2, 16, 64], P(None, 'azim', 'axial'), may hold values from 0 to 2
- decay_rates: float32 [11], replicated, may hold values from 0.3 to 8
Outputs:
- next_state: float32 [11, 4, 4, 4, 16, 64, 128], P(None, None, None, None, 'azim', 'axial')
The draws below stay inside these ranges and needn't reach their ends.
All inputs are finite; a program needn't handle non-finite values.
Results may differ from the reference program's by a relative error of at most 0.0001.
Values sent between devices are 32-bit elements; how exact they have to be, the bound alone decides.
No kernel may reach another device: no remote copies, remote signals or barrier semaphores. Data moves between devices by JAX's collectives and lax.ppermute only.
A program may use at most 128 MiB of HBM per device.

```python
import math
import jax
import jax.numpy as jnp
import numpy as np
from jax import lax

FIELDS = 11
NODES = 4
NR = 128
NA = 16
NX = 64


def set_ends(result, own_key, smallest, largest):
    extent = result.shape
    place = [jax.random.randint(jax.random.fold_in(own_key, axis), (), 0, extent[axis]) for axis in range(len(extent))]
    result = result.at[tuple(place)].set(smallest)
    longest = extent.index(max(extent))
    place[longest] = (place[longest] + 1) % extent[longest]
    return result.at[tuple(place)].set(largest)


def block_scale(rng, extent, pieces, low, high):
    factor_of = 1.0
    for axis_at, shards_of in pieces:
        heights = jax.random.uniform(jax.random.fold_in(jax.random.fold_in(rng, 6), axis_at), (shards_of,), jnp.float32, low / len(pieces), high / len(pieces))
        factor_of = factor_of * jnp.repeat(jnp.exp(heights), extent[axis_at] // shards_of).reshape((-1,) + (1,) * (len(extent) - 1 - axis_at))
    return factor_of


def bell_draw(stream_key, dims, deviation, most, cuts=(), held_as=jnp.bfloat16):
    loudness = block_scale(stream_key, dims, cuts, -0.22, 0.18) if cuts else 1.0
    entries = jax.random.normal(stream_key, dims, jnp.float32) * deviation * loudness
    return jnp.minimum(jnp.maximum(entries, -most), most).astype(held_as)


def setup_inputs(seed: int = 0) -> dict:
    seeds = jax.random.split(jax.random.key(seed), 7)
    flow_state = bell_draw(seeds[0], (FIELDS, NODES, NODES, NODES, NA, NX, NR), 1.0, 6.0, ((4, 16), (5, 8)), jnp.float32)
    velocity = bell_draw(seeds[1], (3, NODES, NODES, NODES, NA, NX, NR), 1.0, 3.0, ((4, 16), (5, 8)), jnp.float32)
    inlet_state = bell_draw(seeds[2], (FIELDS, NODES, NODES, NA, NR), 1.0, 6.0, ((3, 16),), jnp.float32)
    radial_inflow = bell_draw(seeds[3], (2, FIELDS, NODES, NODES, NA, NX), 1.0, 6.0, ((4, 16), (5, 8)), jnp.float32)
    face_tags = set_ends(jax.random.randint(seeds[4], (2, NA, NX), 0, 3), jax.random.fold_in(seeds[4], 1), 0, 2).astype(jnp.int32)
    decay_rates = jnp.clip(jnp.exp(jax.random.uniform(seeds[5], (FIELDS,), jnp.float32, math.log(0.3), math.log(8.0))), 0.3, 8.0)
    return {"flow_state": flow_state, "velocity": velocity, "inlet_state": inlet_state, "radial_inflow": radial_inflow, "face_tags": face_tags, "decay_rates": decay_rates}


time_step = 0.025
metric_scales = (2.0, 1.6, 2.4)
end_lift = 6.0
patterns = ('ij,fjxrpqs->fixrpqs', 'ij,fajrpqs->fairpqs', 'ij,faxjpqs->faxipqs')

def lobatto_derivative():
    points = np.array([-1.0, -1.0 / np.sqrt(5.0), 1.0 / np.sqrt(5.0), 1.0])
    barycentric = np.array([1.0 / np.prod([points[j] - points[k] for k in range(4) if k != j]) for j in range(4)])
    matrix = np.zeros((4, 4))
    for i in range(4):
        for j in range(4):
            if i != j:
                matrix[i, j] = barycentric[j] / barycentric[i] / (points[i] - points[j])
        matrix[i, i] = -np.sum(matrix[i])
    return jnp.asarray(matrix, jnp.float32)

def flux_star(left_states, right_states, fields):
    value_left, speed_left = (left_states[:fields], left_states[fields:])
    value_right, speed_right = (right_states[:fields], right_states[fields:])
    larger = jnp.maximum(jnp.abs(speed_left), jnp.abs(speed_right))
    return 0.5 * (speed_left * value_left + speed_right * value_right) - 0.5 * larger * (value_right - value_left)

def apply_faces(tendency, packed, left_states, right_states, node_dim, elem_dim, metric, fields):
    fluxes = flux_star(left_states, right_states, fields)
    faces_count = left_states.shape[elem_dim]
    upper_flux = lax.slice_in_dim(fluxes, 1, faces_count, axis=elem_dim)
    lower_flux = lax.slice_in_dim(fluxes, 0, faces_count - 1, axis=elem_dim)
    first_face = lax.index_in_dim(packed, 0, node_dim, False)
    last_face = lax.index_in_dim(packed, 3, node_dim, False)
    own_first = first_face[:fields] * first_face[fields:]
    own_last = last_face[:fields] * last_face[fields:]
    index_low = (slice(None),) * node_dim + (0,)
    index_high = (slice(None),) * node_dim + (3,)
    tendency = tendency.at[index_low].add(end_lift * metric * (lower_flux - own_first))
    tendency = tendency.at[index_high].add(-end_lift * metric * (upper_flux - own_last))
    return tendency

def radial_states(packed, face_tags, radial_inflow, fields):
    first_face = packed[:, :, :, 0]
    last_face = packed[:, :, :, 3]

    def outside(boundary, kinds, imposed):
        value = jnp.where(kinds == 1, imposed, boundary[:fields])
        speed = jnp.where(kinds == 0, -boundary[fields:], boundary[fields:])
        return jnp.concatenate([value, speed], 0)
    inner_side = outside(first_face[..., 0], face_tags[0], radial_inflow[0])
    outer_side = outside(last_face[..., -1], face_tags[1], radial_inflow[1])
    left_states = jnp.concatenate([inner_side[..., None], last_face], 5)
    right_states = jnp.concatenate([first_face, outer_side[..., None]], 5)
    return (left_states, right_states)

def tendency_of(flow_state, velocity, inlet_state, radial_inflow, face_tags, decay_rates):
    fields = flow_state.shape[0]
    derivative = lobatto_derivative()
    tendency = -decay_rates.reshape((fields, 1, 1, 1, 1, 1, 1)) * flow_state
    for direction in range(3):
        speed_part = velocity[direction:direction + 1]
        tendency = tendency - metric_scales[direction] * jnp.einsum(patterns[direction], derivative, speed_part * flow_state, precision=lax.Precision.HIGHEST)
        packed = jnp.concatenate([flow_state, speed_part], 0)
        if direction == 0:
            first_face = packed[:, 0]
            last_face = packed[:, 3]
            left_states = jnp.concatenate([last_face[:, :, :, -1:], last_face], 3)
            right_states = jnp.concatenate([first_face, first_face[:, :, :, :1]], 3)
        elif direction == 1:
            first_face = packed[:, :, 0]
            last_face = packed[:, :, 3]
            ghost_in = jnp.concatenate([inlet_state[:, :, :, :, None, :], first_face[fields:, :, :, :, :1]], 0)
            left_states = jnp.concatenate([ghost_in, last_face], 4)
            right_states = jnp.concatenate([first_face, last_face[:, :, :, :, -1:]], 4)
        else:
            left_states, right_states = radial_states(packed, face_tags, radial_inflow, fields)
        tendency = apply_faces(tendency, packed, left_states, right_states, direction + 1, direction + 3, metric_scales[direction], fields)
    return tendency

def reference(flow_state, velocity, inlet_state, radial_inflow, face_tags, decay_rates):
    first_rate = tendency_of(flow_state, velocity, inlet_state, radial_inflow, face_tags, decay_rates)
    section_one = flow_state + time_step * first_rate
    second_rate = tendency_of(section_one, velocity, inlet_state, radial_inflow, face_tags, decay_rates)
    return 0.5 * flow_state + 0.5 * (section_one + time_step * second_rate)
```

```python
import jax
import jax.numpy as jnp
import numpy as np
from jax import lax
from jax.experimental import pallas as pl
from jax.experimental.pallas import tpu as pltpu
from jax.sharding import PartitionSpec as P

time_step = 0.025
metric_scales = (2.0, 1.6, 2.4)
root5 = float(np.sqrt(5.0))
speed_scales = tuple(0.25 * c * time_step for c in metric_scales)
vmem = pl.BlockSpec(memory_space=pltpu.VMEM)
smem = pl.BlockSpec(memory_space=pltpu.SMEM)
anywhere = pl.BlockSpec(memory_space=pl.ANY)
vmem_limit = 40 * 1024 * 1024
tile = (8, 128)


def params():
    return pltpu.CompilerParams(vmem_limit_bytes=vmem_limit)


def arr(*shape):
    return jax.ShapeDtypeStruct(shape, jnp.float32)


def volume(g0, g1, g2, g3):
    e0, o0, e1, o1 = g0 + g3, g0 - g3, g1 + g2, g1 - g2
    h1 = root5 * o1
    s03 = o0 - 5.0 * h1
    d03 = e0 + 5.0 * e1
    s12 = o0 + h1
    d12 = root5 * (e0 - e1)
    return s03 - d03, s12 + d12, s12 - d12, s03 + d03


def face_planes():
    odd = lax.rem(lax.axis_index("azim"), 2)
    return 3 * odd, 3 - 3 * odd


def extract_kernel(u, vel, cross, chip, sems):
    plane_x, plane_c = face_planes()
    fields = u.shape[0]
    copies = []
    for dst, plane in ((cross, plane_x), (chip, plane_c)):
        copies.append((u.at[:, plane], dst.at[pl.ds(0, fields)]))
        copies.append((vel.at[0, plane], dst.at[fields]))
    copies = [pltpu.make_async_copy(s, d, sems.at[i]) for i, (s, d) in enumerate(copies)]
    for c in copies:
        c.start()
    for c in copies:
        c.wait()


def extract(u, vel):
    fields = u.shape[0]
    return pl.pallas_call(
        extract_kernel,
        out_shape=[arr(fields + 1, 16, 8, 128)] * 2,
        in_specs=[anywhere] * 2,
        out_specs=[anywhere] * 2,
        scratch_shapes=[pltpu.SemaphoreType.DMA((4,))],
        compiler_params=params(),
    )(u, vel)


def speeds_and_coefs(vel, tags, va, cax, crad, ghost_l, ghost_r):
    fields = ghost_l.shape[0] - 1
    lane = lax.broadcasted_iota(jnp.int32, tile, 1)
    sub = lax.broadcasted_iota(jnp.int32, tile, 0)
    position = lax.axis_index("axial")
    first = jnp.logical_and(sub == 0, position == 0)
    last = jnp.logical_and(sub == 7, position == lax.axis_size("axial") - 1)
    tag = tags[...]
    inner, outer = lane == 0, lane == 127

    def plane(a, carry):
        for d in range(3):
            for k in range(16):
                va[d, a, k] = vel[d, a, k] * speed_scales[d]
        for r in range(4):
            a0, a3 = va[1, a, r], va[1, a, 12 + r]
            row_l = ghost_l[fields, pl.ds(a * 4 + r, 1), :] * speed_scales[1]
            row_r = ghost_r[fields, pl.ds(a * 4 + r, 1), :] * speed_scales[1]
            below = jnp.where(sub == 0, row_l, pltpu.roll(a3, 1, 0))
            below = jnp.where(first, a0, below)
            above = jnp.where(sub == 7, row_r, pltpu.roll(a0, 7, 0))
            m_low = jnp.maximum(jnp.abs(a0), jnp.abs(below))
            m_up = jnp.maximum(jnp.abs(a3), jnp.abs(above))
            cax[a, r, 0] = -12.0 * m_low
            cax[a, r, 1] = 12.0 * (m_low + below)
            cax[a, r, 2] = jnp.where(last, -12.0 * a3, -12.0 * m_up)
            cax[a, r, 3] = jnp.where(last, 0.0, 12.0 * (m_up - above))
        for x in range(4):
            a0, a3 = va[2, a, 4 * x], va[2, a, 4 * x + 3]
            below = jnp.where(inner, a0, pltpu.roll(a3, 1, 1))
            above = jnp.where(outer, a3, pltpu.roll(a0, 127, 1))
            m_low = jnp.maximum(jnp.abs(a0), jnp.abs(below))
            m_up = jnp.maximum(jnp.abs(a3), jnp.abs(above))
            own_low, out_low = -12.0 * m_low, 12.0 * (m_low + below)
            own_up, out_up = -12.0 * m_up, 12.0 * (m_up - above)
            own_low = jnp.where(inner & (tag == 0), -12.0 * a0, own_low)
            own_low = jnp.where(inner & (tag == 2), 12.0 * a0, own_low)
            own_up = jnp.where(outer & (tag == 0), 12.0 * a3, own_up)
            own_up = jnp.where(outer & (tag == 2), -12.0 * a3, own_up)
            closed = (inner | outer) & (tag != 1)
            crad[a, x, 0] = own_low
            crad[a, x, 1] = jnp.where(inner & closed, 0.0, out_low)
            crad[a, x, 2] = own_up
            crad[a, x, 3] = jnp.where(outer & closed, 0.0, out_up)
        return carry

    lax.fori_loop(0, 4, plane, 0)


def plane_terms(f, a, keep, src, va, cax, crad, edge, ghost_l, ghost_r, edge_f):
    lane = lax.broadcasted_iota(jnp.int32, tile, 1)
    sub = lax.broadcasted_iota(jnp.int32, tile, 0)
    u = [src[f, a, k] for k in range(16)]
    acc = [keep * v for v in u]
    for r in range(4):
        line = [u[4 * x + r] for x in range(4)]
        out = volume(*[va[1, a, 4 * x + r] * line[x] for x in range(4)])
        below = jnp.where(
            sub == 0, ghost_l[edge_f, pl.ds(a * 4 + r, 1), :], pltpu.roll(line[3], 1, 0)
        )
        above = jnp.where(
            sub == 7, ghost_r[edge_f, pl.ds(a * 4 + r, 1), :], pltpu.roll(line[0], 7, 0)
        )
        acc[r] += out[0] + (cax[a, r, 0] * line[0] + cax[a, r, 1] * below)
        acc[4 + r] += out[1]
        acc[8 + r] += out[2]
        acc[12 + r] += out[3] + (cax[a, r, 2] * line[3] + cax[a, r, 3] * above)
    for x in range(4):
        line = [u[4 * x + r] for r in range(4)]
        out = volume(*[va[2, a, 4 * x + r] * line[r] for r in range(4)])
        imposed = edge[edge_f, a * 4 + x]
        below = jnp.where(lane == 0, imposed, pltpu.roll(line[3], 1, 1))
        above = jnp.where(lane == 127, imposed, pltpu.roll(line[0], 127, 1))
        acc[4 * x] += out[0] + (crad[a, x, 0] * line[0] + crad[a, x, 1] * below)
        acc[4 * x + 1] += out[1]
        acc[4 * x + 2] += out[2]
        acc[4 * x + 3] += out[3] + (crad[a, x, 2] * line[3] + crad[a, x, 3] * above)
    return u, acc


def pack_ghosts(inlet, recv_a, recv_b, ghost_l, ghost_r):
    position = lax.axis_index("axial")
    odd = lax.rem(position, 2) == 1
    rows = recv_a.shape[0]
    fields = inlet.shape[0]
    a, b = recv_a[...], recv_b[...]
    lower = jnp.where(odd, a, b)
    ghost_r[pl.ds(0, rows)] = jnp.where(odd, b, a)
    ghost_l[pl.ds(0, fields)] = jnp.where(position == 0, inlet[...], lower[:fields])
    if rows > fields:
        ghost_l[fields] = lower[fields]


def first_kernel(
    decay, tags, edge, inlet, recv_a, recv_b, u, vel, acc, va, cax, crad, ghost_l, ghost_r
):
    fields = u.shape[0]
    pack_ghosts(inlet, recv_a, recv_b, ghost_l, ghost_r)
    speeds_and_coefs(vel, tags, va, cax, crad, ghost_l, ghost_r)

    def field(f, carry):
        keep = 1.0 - time_step * decay[f]

        def plane(a, carry):
            _, out = plane_terms(f, a, keep, u, va, cax, crad, edge, ghost_l, ghost_r, f)
            for k in range(16):
                acc[f, a, k] = out[k]
            return carry

        lax.fori_loop(0, 4, plane, 0)

        def lines(q, carry):
            for r in range(4):
                k = q * 4 + r
                out = volume(*[va[0, a, k] * u[f, a, k] for a in range(4)])
                for a in range(4):
                    acc[f, a, k] += out[a]
            return carry

        lax.fori_loop(0, 4, lines, 0)
        return carry

    lax.fori_loop(0, fields, field, 0)


def first_section(decay, tags, edge, inlet, recv_a, recv_b, u, vel):
    fields = u.shape[0]
    return pl.pallas_call(
        first_kernel,
        out_shape=[
            arr(fields, 4, 16, 8, 128),
            arr(3, 4, 16, 8, 128),
            arr(4, 4, 4, 8, 128),
            arr(4, 4, 4, 8, 128),
        ],
        in_specs=[smem] + [vmem] * 7,
        out_specs=[vmem] * 4,
        scratch_shapes=[pltpu.VMEM((fields + 1, 16, 128), jnp.float32)] * 2,
        compiler_params=params(),
    )(decay, tags, edge, inlet, recv_a, recv_b, u, vel)


def close_kernel(recv_x, recv_c, u, va, acc, s1, send_x, send_c, send_a, send_b, caz):
    fields = u.shape[0]
    planes = face_planes()
    for side, (recv, send) in enumerate(((recv_x, send_x), (recv_c, send_c))):
        plane = planes[side]
        sign = jnp.where(plane == 0, 1.0, -1.0)
        for k in range(16):
            own, other = va[0, plane, k], recv[fields, k] * speed_scales[0]
            m = jnp.maximum(jnp.abs(own), jnp.abs(other))
            caz[plane, k] = -12.0 * m
            caz[plane + 1 - lax.div(plane, 3) * 2, k] = 12.0 * (m + sign * other)

    position = lax.axis_index("axial")
    odd = lax.rem(position, 2) == 1

    def field(f, carry):
        for side, (recv, send) in enumerate(((recv_x, send_x), (recv_c, send_c))):
            plane = planes[side]
            beside = plane + 1 - lax.div(plane, 3) * 2
            for k in range(16):
                value = acc[f, plane, k] + (
                    caz[plane, k] * u[f, plane, k] + caz[beside, k] * recv[f, k]
                )
                s1[f, plane, k] = value
                send[f, k] = value
        for a in (1, 2):
            for k in range(16):
                s1[f, a, k] = acc[f, a, k]
        for a in range(4):
            for r in range(4):
                low = s1[f, a, r, pl.ds(0, 1), :]
                high = s1[f, a, 12 + r, pl.ds(7, 1), :]
                send_a[f, pl.ds(a * 4 + r, 1), :] = jnp.where(odd, low, high)
                send_b[f, pl.ds(a * 4 + r, 1), :] = jnp.where(odd, high, low)
        return carry

    lax.fori_loop(0, fields, field, 0)


def close_first(recv_x, recv_c, u, va, acc):
    fields = u.shape[0]
    return pl.pallas_call(
        close_kernel,
        out_shape=[
            arr(fields, 4, 16, 8, 128),
            arr(fields, 16, 8, 128),
            arr(fields, 16, 8, 128),
            arr(fields, 16, 128),
            arr(fields, 16, 128),
            arr(4, 16, 8, 128),
        ],
        in_specs=[vmem] * 5,
        out_specs=[vmem] * 6,
        compiler_params=params(),
    )(recv_x, recv_c, u, va, acc)


def second_kernel(
    decay, edge, inlet, recv_a, recv_b, u, s1, va, cax, crad, caz, part, ghost_l, ghost_r
):
    fields = u.shape[0]
    pack_ghosts(inlet, recv_a, recv_b, ghost_l, ghost_r)

    def field(f, carry):
        keep = 1.0 - time_step * decay[f]

        def plane(a, carry):
            _, out = plane_terms(f, a, keep, s1, va, cax, crad, edge, ghost_l, ghost_r, f)
            for k in range(16):
                part[f, a, k] = 0.5 * (u[f, a, k] + out[k])
            return carry

        lax.fori_loop(0, 4, plane, 0)

        def lines(q, carry):
            for r in range(4):
                k = q * 4 + r
                line = [s1[f, a, k] for a in range(4)]
                out = list(volume(*[va[0, a, k] * line[a] for a in range(4)]))
                out[0] += caz[0, k] * line[0]
                out[3] += caz[3, k] * line[3]
                for a in range(4):
                    part[f, a, k] += 0.5 * out[a]
            return carry

        lax.fori_loop(0, 4, lines, 0)
        return carry

    lax.fori_loop(0, fields, field, 0)


def second_section(decay, edge, inlet, recv_a, recv_b, u, s1, va, cax, crad, caz):
    fields = u.shape[0]
    return pl.pallas_call(
        second_kernel,
        out_shape=arr(fields, 4, 16, 8, 128),
        in_specs=[smem] + [vmem] * 10,
        out_specs=vmem,
        scratch_shapes=[pltpu.VMEM((fields, 16, 128), jnp.float32)] * 2,
        compiler_params=params(),
    )(decay, edge, inlet, recv_a, recv_b, u, s1, va, cax, crad, caz)


def finish_kernel(recv_x, recv_c, caz, part, out):
    fields = part.shape[0]
    planes = face_planes()

    def field(f, carry):
        for side, recv in enumerate((recv_x, recv_c)):
            plane = planes[side]
            beside = plane + 1 - lax.div(plane, 3) * 2
            for k in range(16):
                out[f, plane, k] = part[f, plane, k] + 0.5 * (caz[beside, k] * recv[f, k])
        for a in (1, 2):
            for k in range(16):
                out[f, a, k] = part[f, a, k]
        return carry

    lax.fori_loop(0, fields, field, 0)


def finish(recv_x, recv_c, caz, part):
    return pl.pallas_call(
        finish_kernel,
        out_shape=arr(*part.shape),
        in_specs=[vmem] * 4,
        out_specs=vmem,
        compiler_params=params(),
    )(recv_x, recv_c, caz, part)


def swap(array, axis, odd_up):
    count = lax.axis_size(axis)
    if odd_up:
        route = [(i, (i + 1) % count if i % 2 else (i - 1) % count) for i in range(count)]
    else:
        route = [(i, i ^ 1) for i in range(count)]
    return lax.ppermute(array, axis, route)


def per_device(flow_state, velocity, inlet_state, radial_inflow, face_tags, decay_rates):
    fields = flow_state.shape[0]
    u = flow_state.reshape((fields, 4, 16) + tile)
    vel = velocity.reshape((3, 4, 16) + tile)
    inlet = inlet_state.reshape(fields, 16, 128)
    lane = lax.broadcasted_iota(jnp.int32, tile, 1)
    tags = jnp.where(lane == 0, face_tags[0].reshape(8, 1), face_tags[1].reshape(8, 1))
    edges = radial_inflow.reshape(2, fields, 16, 8, 1)
    edge = jnp.where(lane == 0, edges[0], edges[1])

    send_x, send_c = extract(u, vel)
    odd = lax.rem(lax.axis_index("axial"), 2) == 1
    stack = jnp.concatenate(
        [flow_state[:, :, :, :, 0], velocity[1:2, :, :, :, 0]], 0
    )
    low = stack[:, :, 0, :, 0, :].reshape(fields + 1, 16, 128)
    high = stack[:, :, 3, :, 7, :].reshape(fields + 1, 16, 128)
    send_a = jnp.where(odd, low, high)
    send_b = jnp.where(odd, high, low)

    recv_x = swap(send_x, "azim", True)
    recv_c = swap(send_c, "azim", False)
    recv_a = swap(send_a, "axial", False)
    recv_b = swap(send_b, "axial", True)

    acc, va, cax, crad = first_section(
        decay_rates, tags, edge, inlet, recv_a, recv_b, u, vel
    )
    s1, send_x, send_c, send_a, send_b, caz = close_first(recv_x, recv_c, u, va, acc)

    recv_x = swap(send_x, "azim", True)
    recv_c = swap(send_c, "azim", False)
    recv_a = swap(send_a, "axial", False)
    recv_b = swap(send_b, "axial", True)

    part = second_section(
        decay_rates, edge, inlet, recv_a, recv_b, u, s1, va, cax, crad, caz
    )
    out = finish(recv_x, recv_c, caz, part)
    return out.reshape(flow_state.shape)


def solution(mesh):
    in_specs = (
        P(None, None, None, None, "azim", "axial", None),
        P(None, None, None, None, "azim", "axial", None),
        P(None, None, None, "azim", None),
        P(None, None, None, None, "azim", "axial"),
        P(None, "azim", "axial"),
        P(),
    )
    out_specs = P(None, None, None, None, "azim", "axial", None)
    return jax.shard_map(
        per_device, mesh=mesh, in_specs=in_specs, out_specs=out_specs, check_vma=False
    )
```

```python
import jax
import jax.numpy as jnp
import numpy as np
from jax import lax
from jax.experimental import pallas as pl
from jax.experimental.pallas import tpu as pltpu
from jax.sharding import PartitionSpec as P

time_step = 0.025
metric_scales = (2.0, 1.6, 2.4)
root5 = float(np.sqrt(5.0))
speed_scales = tuple(0.25 * c * time_step for c in metric_scales)
vmem = pl.BlockSpec(memory_space=pltpu.VMEM)
smem = pl.BlockSpec(memory_space=pltpu.SMEM)
anywhere = pl.BlockSpec(memory_space=pl.ANY)
in_hbm = pl.BlockSpec(memory_space=pltpu.HBM)
vmem_limit = 40 * 1024 * 1024
tile = (8, 128)


def params(limit=vmem_limit):
    return pltpu.CompilerParams(vmem_limit_bytes=limit)


def arr(*shape):
    return jax.ShapeDtypeStruct(shape, jnp.float32)


def volume(g0, g1, g2, g3):
    e0, o0, e1, o1 = g0 + g3, g0 - g3, g1 + g2, g1 - g2
    h1 = root5 * o1
    s03 = o0 - 5.0 * h1
    d03 = e0 + 5.0 * e1
    s12 = o0 + h1
    d12 = root5 * (e0 - e1)
    return s03 - d03, s12 + d12, s12 - d12, s03 + d03


def face_planes():
    odd = lax.rem(lax.axis_index("azim"), 2)
    return 3 * odd, 3 - 3 * odd


def extract_kernel(u, vel, cross, chip, vel_out, sems):
    fields = u.shape[0]
    sides = list(zip((cross, chip), face_planes()))
    copies = [(vel, vel_out)]
    copies += [(vel.at[0, plane], dst.at[fields]) for dst, plane in sides]
    copies = [pltpu.make_async_copy(s, d, sems.at[i]) for i, (s, d) in enumerate(copies)]
    for c in copies:
        c.start()

    def field(f, carry):
        for dst, plane in sides:
            values = [u[f, plane, k] for k in range(16)]
            for k in range(16):
                dst[f, k] = values[k]
        return carry

    lax.fori_loop(0, fields, field, 0)
    for c in copies:
        c.wait()


def extract(u, vel):
    fields = u.shape[0]
    return pl.pallas_call(
        extract_kernel,
        out_shape=[arr(fields + 1, 16, 8, 128)] * 2 + [arr(*vel.shape)],
        in_specs=[vmem, anywhere],
        out_specs=[vmem] * 3,
        scratch_shapes=[pltpu.SemaphoreType.DMA((3,))],
        compiler_params=params(),
    )(u, vel)


def axial_odd():
    return lax.rem(lax.axis_index("axial"), 2) == 1


def rows_kernel(u, vel, send_a, send_b):
    fields = u.shape[0]
    odd = axial_odd()

    def put(f, a, low, high):
        for r in range(4):
            k = a * 4 + r
            send_a[f, k : k + 1, :] = jnp.where(odd, low[r], high[r])
            send_b[f, k : k + 1, :] = jnp.where(odd, high[r], low[r])

    def field(f, carry):
        for a in range(4):
            put(
                f,
                a,
                [u[f, a, r, 0:1, :] for r in range(4)],
                [u[f, a, 12 + r, 7:8, :] for r in range(4)],
            )
        return carry

    lax.fori_loop(0, fields, field, 0)
    for a in range(4):
        put(
            fields,
            a,
            [vel[1, a, r, 0:1, :] * speed_scales[1] for r in range(4)],
            [vel[1, a, 12 + r, 7:8, :] * speed_scales[1] for r in range(4)],
        )


def rows(u, vel):
    fields = u.shape[0]
    return pl.pallas_call(
        rows_kernel,
        out_shape=[arr(fields + 1, 16, 128)] * 2,
        in_specs=[vmem] * 2,
        out_specs=[vmem] * 2,
        compiler_params=params(),
    )(u, vel)


def prepare_kernel(tags, vel, va, cax, crad):
    lane = lax.broadcasted_iota(jnp.int32, tile, 1)
    sub = lax.broadcasted_iota(jnp.int32, tile, 0)
    tag = tags[...]
    inner, outer = lane == 0, lane == 127

    def plane(a, carry):
        for d in range(3):
            for k in range(16):
                va[d, a, k] = vel[d, a, k] * speed_scales[d]
        for r in range(4):
            a0, a3 = va[1, a, r], va[1, a, 12 + r]
            below, above = pltpu.roll(a3, 1, 0), pltpu.roll(a0, 7, 0)
            m_low = jnp.maximum(jnp.abs(a0), jnp.abs(below))
            m_up = jnp.maximum(jnp.abs(a3), jnp.abs(above))
            cax[a, r, 0] = jnp.where(sub == 0, 0.0, -12.0 * m_low)
            cax[a, r, 1] = jnp.where(sub == 0, 0.0, 12.0 * (m_low + below))
            cax[a, r, 2] = jnp.where(sub == 7, 0.0, -12.0 * m_up)
            cax[a, r, 3] = jnp.where(sub == 7, 0.0, 12.0 * (m_up - above))
        for x in range(4):
            a0, a3 = va[2, a, 4 * x], va[2, a, 4 * x + 3]
            below = jnp.where(inner, a0, pltpu.roll(a3, 1, 1))
            above = jnp.where(outer, a3, pltpu.roll(a0, 127, 1))
            m_low = jnp.maximum(jnp.abs(a0), jnp.abs(below))
            m_up = jnp.maximum(jnp.abs(a3), jnp.abs(above))
            own_low, out_low = -12.0 * m_low, 12.0 * (m_low + below)
            own_up, out_up = -12.0 * m_up, 12.0 * (m_up - above)
            own_low = jnp.where(inner & (tag == 0), -12.0 * a0, own_low)
            own_low = jnp.where(inner & (tag == 2), 12.0 * a0, own_low)
            own_up = jnp.where(outer & (tag == 0), 12.0 * a3, own_up)
            own_up = jnp.where(outer & (tag == 2), -12.0 * a3, own_up)
            crad[a, x, 0] = own_low
            crad[a, x, 1] = jnp.where(inner & (tag != 1), 0.0, out_low)
            crad[a, x, 2] = own_up
            crad[a, x, 3] = jnp.where(outer & (tag != 1), 0.0, out_up)
        return carry

    lax.fori_loop(0, 4, plane, 0)


def prepare(tags, vel):
    return pl.pallas_call(
        prepare_kernel,
        out_shape=[arr(3, 4, 16, 8, 128), arr(4, 4, 4, 8, 128), arr(4, 4, 4, 8, 128)],
        in_specs=[vmem] * 2,
        out_specs=[vmem] * 3,
        compiler_params=params(),
    )(tags, vel)


def plane_terms(f, a, keep, src, va, cax, crad, edge):
    lane = lax.broadcasted_iota(jnp.int32, tile, 1)
    u = [src[f, a, k] for k in range(16)]
    acc = [keep * v for v in u]
    for r in range(4):
        line = [u[4 * x + r] for x in range(4)]
        out = volume(*[va[1, a, 4 * x + r] * line[x] for x in range(4)])
        below, above = pltpu.roll(line[3], 1, 0), pltpu.roll(line[0], 7, 0)
        acc[r] += out[0] + (cax[a, r, 0] * line[0] + cax[a, r, 1] * below)
        acc[4 + r] += out[1]
        acc[8 + r] += out[2]
        acc[12 + r] += out[3] + (cax[a, r, 2] * line[3] + cax[a, r, 3] * above)
    for x in range(4):
        line = [u[4 * x + r] for r in range(4)]
        out = volume(*[va[2, a, 4 * x + r] * line[r] for r in range(4)])
        imposed = edge[f, a * 4 + x]
        below = jnp.where(lane == 0, imposed, pltpu.roll(line[3], 1, 1))
        above = jnp.where(lane == 127, imposed, pltpu.roll(line[0], 127, 1))
        acc[4 * x] += out[0] + (crad[a, x, 0] * line[0] + crad[a, x, 1] * below)
        acc[4 * x + 1] += out[1]
        acc[4 * x + 2] += out[2]
        acc[4 * x + 3] += out[3] + (crad[a, x, 2] * line[3] + crad[a, x, 3] * above)
    return acc


def first_kernel(decay, edge, u, va, cax, crad, acc):
    fields = u.shape[0]

    def field(f, carry):
        keep = 1.0 - time_step * decay[f]
        for q in range(4):
            outs = []
            for k in range(4 * q, 4 * q + 4):
                outs.append(volume(*[va[0, a, k] * u[f, a, k] for a in range(4)]))
            for r in range(4):
                for a in range(4):
                    acc[f, a, 4 * q + r] = outs[r][a]
        for a in range(4):
            out = plane_terms(f, a, keep, u, va, cax, crad, edge)
            for k in range(16):
                acc[f, a, k] += out[k]
        return carry

    lax.fori_loop(0, fields, field, 0)


def first_section(decay, edge, u, va, cax, crad):
    fields = u.shape[0]
    return pl.pallas_call(
        first_kernel,
        out_shape=arr(fields, 4, 16, 8, 128),
        in_specs=[smem] + [vmem] * 5,
        out_specs=vmem,
        compiler_params=params(),
    )(decay, edge, u, va, cax, crad)


def second_kernel(decay, edge, u, s1, va, cax, crad, caz, part):
    fields = u.shape[0]

    def field(f, carry):
        keep = 1.0 - time_step * decay[f]
        for q in range(4):
            outs = []
            for k in range(4 * q, 4 * q + 4):
                line = [s1[f, a, k] for a in range(4)]
                out = list(volume(*[va[0, a, k] * line[a] for a in range(4)]))
                out[0] += caz[0, k] * line[0]
                out[3] += caz[3, k] * line[3]
                outs.append(out)
            for r in range(4):
                for a in range(4):
                    part[f, a, 4 * q + r] = outs[r][a]
        for a in range(4):
            out = plane_terms(f, a, keep, s1, va, cax, crad, edge)
            for k in range(16):
                part[f, a, k] = 0.5 * (u[f, a, k] + (part[f, a, k] + out[k]))
        return carry

    lax.fori_loop(0, fields, field, 0)


def second_section(decay, edge, u, s1, va, cax, crad, caz):
    fields = u.shape[0]
    return pl.pallas_call(
        second_kernel,
        out_shape=arr(fields, 4, 16, 8, 128),
        in_specs=[smem] + [vmem] * 7,
        out_specs=vmem,
        compiler_params=params(),
    )(decay, edge, u, s1, va, cax, crad, caz)


def edge_terms(inlet, own_a, own_b, recv_a, recv_b, factors, low, high):
    position = lax.axis_index("axial")
    odd = axial_odd()
    fields = inlet.shape[0]
    own_low = jnp.where(odd, own_a[...], own_b[...])
    own_high = jnp.where(odd, own_b[...], own_a[...])
    below = jnp.where(odd, recv_a[...], recv_b[...])
    above = jnp.where(odd, recv_b[...], recv_a[...])
    if own_a.shape[0] > fields:
        a0, a3 = own_low[fields], own_high[fields]
        a_below = jnp.where(position == 0, a0, below[fields])
        a_above = above[fields]
        is_last = position == lax.axis_size("axial") - 1
        m_low = jnp.maximum(jnp.abs(a0), jnp.abs(a_below))
        m_up = jnp.maximum(jnp.abs(a3), jnp.abs(a_above))
        factors[0] = -12.0 * m_low
        factors[1] = 12.0 * (m_low + a_below)
        factors[2] = jnp.where(is_last, -12.0 * a3, -12.0 * m_up)
        factors[3] = jnp.where(is_last, 0.0, 12.0 * (m_up - a_above))
    from_below = jnp.where(position == 0, inlet[...], below[:fields])
    low[...] = factors[0] * own_low[:fields] + factors[1] * from_below
    high[...] = factors[2] * own_high[:fields] + factors[3] * above[:fields]
    if own_a.shape[0] == fields:
        low[...] = 0.5 * low[...]
        high[...] = 0.5 * high[...]


def close_kernel(
    inlet, own_a, own_b, recv_a, recv_b, recv_x, recv_c, u, va, acc,
    s1, send_x, send_c, caz, low, high, factors,
):
    fields = u.shape[0]
    sub = lax.broadcasted_iota(jnp.int32, tile, 0)
    planes = face_planes()
    edge_terms(inlet, own_a, own_b, recv_a, recv_b, factors, low, high)
    for side, recv in enumerate((recv_x, recv_c)):
        plane = planes[side]
        sign = jnp.where(plane == 0, 1.0, -1.0)
        beside = plane + 1 - lax.div(plane, 3) * 2
        for k in range(16):
            own, other = va[0, plane, k], recv[fields, k] * speed_scales[0]
            m = jnp.maximum(jnp.abs(own), jnp.abs(other))
            caz[plane, k] = -12.0 * m
            caz[beside, k] = 12.0 * (m + sign * other)

    def field(f, carry):
        for side, (recv, send) in enumerate(((recv_x, send_x), (recv_c, send_c))):
            plane = planes[side]
            beside = plane + 1 - lax.div(plane, 3) * 2
            values = []
            for k in range(16):
                value = acc[f, plane, k] + (
                    caz[plane, k] * u[f, plane, k] + caz[beside, k] * recv[f, k]
                )
                if k < 4:
                    row = low[f, pl.ds(plane * 4 + k, 1), :]
                    value += jnp.where(sub == 0, row, 0.0)
                if k >= 12:
                    row = high[f, pl.ds(plane * 4 + k - 12, 1), :]
                    value += jnp.where(sub == 7, row, 0.0)
                values.append(value)
            for k in range(16):
                s1[f, plane, k] = values[k]
                send[f, k] = values[k]
        return carry

    lax.fori_loop(0, fields, field, 0)


def close_first(inlet, own_a, own_b, recv_a, recv_b, recv_x, recv_c, u, va, acc):
    fields = u.shape[0]
    return pl.pallas_call(
        close_kernel,
        out_shape=[
            arr(fields, 4, 16, 8, 128),
            arr(fields, 16, 8, 128),
            arr(fields, 16, 8, 128),
            arr(4, 16, 8, 128),
            arr(fields, 16, 128),
            arr(fields, 16, 128),
            arr(4, 16, 128),
        ],
        in_specs=[vmem] * 10,
        out_specs=[vmem] * 7,
        input_output_aliases={9: 0},
        compiler_params=params(),
    )(inlet, own_a, own_b, recv_a, recv_b, recv_x, recv_c, u, va, acc)


def middle_kernel(low, high, s1_in, s1, send_a, send_b):
    fields = s1.shape[0]
    odd = axial_odd()

    def field(f, carry):
        for a in range(4):
            for r in range(4):
                k = a * 4 + r
                first = s1_in[f, a, r, 0:1, :]
                last = s1_in[f, a, 12 + r, 7:8, :]
                if a in (1, 2):
                    first += low[f, k : k + 1, :]
                    last += high[f, k : k + 1, :]
                    s1[f, a, r, 0:1, :] = first
                    s1[f, a, 12 + r, 7:8, :] = last
                send_a[f, k : k + 1, :] = jnp.where(odd, first, last)
                send_b[f, k : k + 1, :] = jnp.where(odd, last, first)
        return carry

    lax.fori_loop(0, fields, field, 0)


def middle(low, high, s1):
    fields = s1.shape[0]
    return pl.pallas_call(
        middle_kernel,
        out_shape=[arr(*s1.shape), arr(fields, 16, 128), arr(fields, 16, 128)],
        in_specs=[vmem] * 3,
        out_specs=[vmem] * 3,
        input_output_aliases={2: 0},
        compiler_params=params(),
    )(low, high, s1)


def finish_kernel(
    inlet, own_a, own_b, recv_a, recv_b, factors, recv_x, recv_c, caz, part,
    out, low, high, work, sems,
):
    fields = part.shape[0]
    sub = lax.broadcasted_iota(jnp.int32, tile, 0)
    planes = face_planes()
    edge_terms(inlet, own_a, own_b, recv_a, recv_b, factors, low, high)

    def field(f, carry):
        def edged(a, k, value):
            if k < 4:
                row = low[f, pl.ds(a * 4 + k, 1), :]
                return value + jnp.where(sub == 0, row, 0.0)
            if k >= 12:
                row = high[f, pl.ds(a * 4 + k - 12, 1), :]
                return value + jnp.where(sub == 7, row, 0.0)
            return value

        for side, recv in enumerate((recv_x, recv_c)):
            plane = planes[side]
            beside = plane + 1 - lax.div(plane, 3) * 2
            values = []
            for k in range(16):
                value = part[f, plane, k] + 0.5 * (caz[beside, k] * recv[f, k])
                values.append(edged(plane, k, value))
            for k in range(16):
                work[f, plane, k] = values[k]
        for a in (1, 2):
            values = [edged(a, k, part[f, a, k]) for k in range(16)]
            for k in range(16):
                work[f, a, k] = values[k]
        pltpu.make_async_copy(work.at[f], out.at[f], sems.at[f]).start()
        return carry

    lax.fori_loop(0, fields, field, 0)

    def drain(f, carry):
        pltpu.make_async_copy(work.at[f], out.at[f], sems.at[f]).wait()
        return carry

    lax.fori_loop(0, fields, drain, 0)


def finish(inlet, own_a, own_b, recv_a, recv_b, factors, recv_x, recv_c, caz, part):
    fields = part.shape[0]
    return pl.pallas_call(
        finish_kernel,
        out_shape=arr(*part.shape),
        in_specs=[vmem] * 10,
        out_specs=in_hbm,
        scratch_shapes=[
            pltpu.VMEM((fields, 16, 128), jnp.float32),
            pltpu.VMEM((fields, 16, 128), jnp.float32),
            pltpu.VMEM(part.shape, jnp.float32),
            pltpu.SemaphoreType.DMA((fields,)),
        ],
        compiler_params=params(),
    )(inlet, own_a, own_b, recv_a, recv_b, factors, recv_x, recv_c, caz, part)


def swap(array, axis, odd_up):
    count = lax.axis_size(axis)
    if odd_up:
        route = [(i, (i + 1) % count if i % 2 else (i - 1) % count) for i in range(count)]
    else:
        route = [(i, i ^ 1) for i in range(count)]
    return lax.ppermute(array, axis, route)


def per_device(flow_state, velocity, inlet_state, radial_inflow, face_tags, decay_rates):
    fields = flow_state.shape[0]
    u = flow_state.reshape((fields, 4, 16) + tile)
    vel = velocity.reshape((3, 4, 16) + tile)
    inlet = inlet_state.reshape(fields, 16, 128)
    lane = lax.broadcasted_iota(jnp.int32, tile, 1)
    tags = jnp.where(lane == 0, face_tags[0].reshape(8, 1), face_tags[1].reshape(8, 1))
    edges = radial_inflow.reshape(2, fields, 16, 8, 1)
    edge = jnp.where(lane == 0, edges[0], edges[1])

    send_x, send_c, vel = extract(u, vel)
    recv_x = swap(send_x, "azim", True)
    recv_c = swap(send_c, "azim", False)
    u_held, _, _ = lax.optimization_barrier((u, send_x, send_c))
    own_a, own_b = rows(u_held, vel)
    recv_a = swap(own_a, "axial", False)
    recv_b = swap(own_b, "axial", True)

    va, cax, crad = prepare(tags, vel)
    acc = first_section(decay_rates, edge, u, va, cax, crad)
    s1, send_x, send_c, caz, low, high, factors = close_first(
        inlet, own_a, own_b, recv_a, recv_b, recv_x, recv_c, u, va, acc
    )
    recv_x = swap(send_x, "azim", True)
    recv_c = swap(send_c, "azim", False)
    s1, own_a, own_b = middle(low, high, s1)
    recv_a = swap(own_a, "axial", False)
    recv_b = swap(own_b, "axial", True)

    part = second_section(decay_rates, edge, u, s1, va, cax, crad, caz)
    out = finish(inlet, own_a, own_b, recv_a, recv_b, factors, recv_x, recv_c, caz, part)
    return out.reshape(flow_state.shape)


def solution(mesh):
    in_specs = (
        P(None, None, None, None, "azim", "axial", None),
        P(None, None, None, None, "azim", "axial", None),
        P(None, None, None, "azim", None),
        P(None, None, None, None, "azim", "axial"),
        P(None, "azim", "axial"),
        P(),
    )
    out_specs = P(None, None, None, None, "azim", "axial", None)
    return jax.shard_map(
        per_device, mesh=mesh, in_specs=in_specs, out_specs=out_specs, check_vma=False
    )
```

```python
import functools

import jax
import jax.numpy as jnp
import numpy as np
from jax import lax
from jax.experimental import pallas as pl
from jax.experimental.pallas import tpu as pltpu
from jax.sharding import PartitionSpec as P

time_step = 0.025
metric_scales = (2.0, 1.6, 2.4)
root5 = float(np.sqrt(5.0))
speed_scales = tuple(0.25 * c * time_step for c in metric_scales)
vmem = pl.BlockSpec(memory_space=pltpu.VMEM)
smem = pl.BlockSpec(memory_space=pltpu.SMEM)
anywhere = pl.BlockSpec(memory_space=pl.ANY)
in_hbm = pl.BlockSpec(memory_space=pltpu.HBM)
vmem_limit = 16 * 1024 * 1024
tile = (8, 128)


def params(limit=vmem_limit):
    return pltpu.CompilerParams(vmem_limit_bytes=limit)


def arr(*shape):
    return jax.ShapeDtypeStruct(shape, jnp.float32)


def volume(g0, g1, g2, g3):
    e0, o0, e1, o1 = g0 + g3, g0 - g3, g1 + g2, g1 - g2
    h1 = root5 * o1
    s03 = o0 - 5.0 * h1
    d03 = e0 + 5.0 * e1
    s12 = o0 + h1
    d12 = root5 * (e0 - e1)
    return s03 - d03, s12 + d12, s12 - d12, s03 + d03


def depart_kernel(u, vel, rows_low, rows_high, face_low, face_high):
    fields = u.shape[0]

    def put(f, a, low, high):
        for r in range(4):
            k = a * 4 + r
            rows_low[f, k : k + 1, :] = low[r]
            rows_high[f, k : k + 1, :] = high[r]

    def field(f, carry):
        for a in range(4):
            put(
                f,
                a,
                [u[f, a, r, 0:1, :] for r in range(4)],
                [u[f, a, 12 + r, 7:8, :] for r in range(4)],
            )
        for dst, plane in ((face_low, 0), (face_high, 3)):
            values = [u[f, plane, k] for k in range(16)]
            for k in range(16):
                dst[f, k] = values[k]
        return carry

    lax.fori_loop(0, fields, field, 0)
    for a in range(4):
        put(
            fields,
            a,
            [vel[1, a, r, 0:1, :] * speed_scales[1] for r in range(4)],
            [vel[1, a, 12 + r, 7:8, :] * speed_scales[1] for r in range(4)],
        )
    for dst, plane in ((face_low, 0), (face_high, 3)):
        values = [vel[0, plane, k] * speed_scales[0] for k in range(16)]
        for k in range(16):
            dst[fields, k] = values[k]


def depart(u, vel):
    fields = u.shape[0]
    return pl.pallas_call(
        depart_kernel,
        out_shape=[arr(fields + 1, 16, 128)] * 2 + [arr(fields + 1, 16, 8, 128)] * 2,
        in_specs=[vmem] * 2,
        out_specs=[vmem] * 4,
        compiler_params=params(),
    )(u, vel)


def prepare_kernel(tags, inflow, vel, va, cax, crad, edge):
    lane = lax.broadcasted_iota(jnp.int32, tile, 1)
    sub = lax.broadcasted_iota(jnp.int32, tile, 0)
    tag = tags[...]
    inner, outer = lane == 0, lane == 127

    def imposed(k, carry):
        within, beyond = inflow[0, k], inflow[1, k]
        for f in range(edge.shape[0]):
            edge[f, k] = jnp.where(inner, within[:, f : f + 1], beyond[:, f : f + 1])
        return carry

    lax.fori_loop(0, 16, imposed, 0)

    def plane(a, carry):
        for d in range(3):
            for k in range(16):
                va[d, a, k] = vel[d, a, k] * speed_scales[d]
        for r in range(4):
            a0, a3 = va[1, a, r], va[1, a, 12 + r]
            below, above = pltpu.roll(a3, 1, 0), pltpu.roll(a0, 7, 0)
            m_low = jnp.maximum(jnp.abs(a0), jnp.abs(below))
            m_up = jnp.maximum(jnp.abs(a3), jnp.abs(above))
            cax[a, r, 0] = jnp.where(sub == 0, 0.0, -12.0 * m_low)
            cax[a, r, 1] = jnp.where(sub == 0, 0.0, 12.0 * (m_low + below))
            cax[a, r, 2] = jnp.where(sub == 7, 0.0, -12.0 * m_up)
            cax[a, r, 3] = jnp.where(sub == 7, 0.0, 12.0 * (m_up - above))
        for x in range(4):
            a0, a3 = va[2, a, 4 * x], va[2, a, 4 * x + 3]
            below = jnp.where(inner, a0, pltpu.roll(a3, 1, 1))
            above = jnp.where(outer, a3, pltpu.roll(a0, 127, 1))
            m_low = jnp.maximum(jnp.abs(a0), jnp.abs(below))
            m_up = jnp.maximum(jnp.abs(a3), jnp.abs(above))
            own_low, out_low = -12.0 * m_low, 12.0 * (m_low + below)
            own_up, out_up = -12.0 * m_up, 12.0 * (m_up - above)
            own_low = jnp.where(inner & (tag == 0), -12.0 * a0, own_low)
            own_low = jnp.where(inner & (tag == 2), 12.0 * a0, own_low)
            own_up = jnp.where(outer & (tag == 0), 12.0 * a3, own_up)
            own_up = jnp.where(outer & (tag == 2), -12.0 * a3, own_up)
            crad[a, x, 0] = own_low
            crad[a, x, 1] = jnp.where(inner & (tag != 1), 0.0, out_low)
            crad[a, x, 2] = own_up
            crad[a, x, 3] = jnp.where(outer & (tag != 1), 0.0, out_up)
        return carry

    lax.fori_loop(0, 4, plane, 0)


def prepare(tags, inflow, vel):
    return pl.pallas_call(
        prepare_kernel,
        out_shape=[
            arr(3, 4, 16, 8, 128),
            arr(4, 4, 4, 8, 128),
            arr(4, 4, 4, 8, 128),
            arr(inflow.shape[-1], 16, 8, 128),
        ],
        in_specs=[vmem] * 3,
        out_specs=[vmem] * 4,
        compiler_params=params(),
    )(tags, inflow, vel)


def plane_terms(f, a, keep, src, va, cax, crad, edge):
    lane = lax.broadcasted_iota(jnp.int32, tile, 1)
    u = [src[f, a, k] for k in range(16)]
    acc = [keep * v for v in u]
    for r in range(4):
        line = [u[4 * x + r] for x in range(4)]
        out = volume(*[va[1, a, 4 * x + r] * line[x] for x in range(4)])
        below, above = pltpu.roll(line[3], 1, 0), pltpu.roll(line[0], 7, 0)
        acc[r] += out[0] + (cax[a, r, 0] * line[0] + cax[a, r, 1] * below)
        acc[4 + r] += out[1]
        acc[8 + r] += out[2]
        acc[12 + r] += out[3] + (cax[a, r, 2] * line[3] + cax[a, r, 3] * above)
    for x in range(4):
        line = [u[4 * x + r] for r in range(4)]
        out = volume(*[va[2, a, 4 * x + r] * line[r] for r in range(4)])
        imposed = edge[f, a * 4 + x]
        below = jnp.where(lane == 0, imposed, pltpu.roll(line[3], 1, 1))
        above = jnp.where(lane == 127, imposed, pltpu.roll(line[0], 127, 1))
        acc[4 * x] += out[0] + (crad[a, x, 0] * line[0] + crad[a, x, 1] * below)
        acc[4 * x + 1] += out[1]
        acc[4 * x + 2] += out[2]
        acc[4 * x + 3] += out[3] + (crad[a, x, 2] * line[3] + crad[a, x, 3] * above)
    return acc


def first_kernel(decay, edge, u, va, cax, crad, acc):
    fields = u.shape[0]

    def field(f, carry):
        keep = 1.0 - time_step * decay[f]
        for q in range(4):
            outs = []
            for k in range(4 * q, 4 * q + 4):
                outs.append(volume(*[va[0, a, k] * u[f, a, k] for a in range(4)]))
            for r in range(4):
                for a in range(4):
                    acc[f, a, 4 * q + r] = outs[r][a]
        for a in range(4):
            out = plane_terms(f, a, keep, u, va, cax, crad, edge)
            for k in range(16):
                acc[f, a, k] += out[k]
        return carry

    lax.fori_loop(0, fields, field, 0)


def first_section(decay, edge, u, va, cax, crad):
    fields = u.shape[0]
    return pl.pallas_call(
        first_kernel,
        out_shape=arr(fields, 4, 16, 8, 128),
        in_specs=[smem] + [vmem] * 5,
        out_specs=vmem,
        compiler_params=params(),
    )(decay, edge, u, va, cax, crad)


def second_kernel(decay, edge, u, s1, va, cax, crad, caz, part):
    fields = u.shape[0]

    def field(f, carry):
        keep = 1.0 - time_step * decay[f]
        for q in range(4):
            outs = []
            for k in range(4 * q, 4 * q + 4):
                line = [s1[f, a, k] for a in range(4)]
                out = list(volume(*[va[0, a, k] * line[a] for a in range(4)]))
                out[0] += caz[0, k] * line[0]
                out[3] += caz[3, k] * line[3]
                outs.append(out)
            for r in range(4):
                for a in range(4):
                    part[f, a, 4 * q + r] = outs[r][a]
        for a in range(4):
            out = plane_terms(f, a, keep, s1, va, cax, crad, edge)
            for k in range(16):
                part[f, a, k] = 0.5 * (u[f, a, k] + (part[f, a, k] + out[k]))
        return carry

    lax.fori_loop(0, fields, field, 0)


def second_section(decay, edge, u, s1, va, cax, crad, caz):
    fields = u.shape[0]
    return pl.pallas_call(
        second_kernel,
        out_shape=arr(fields, 4, 16, 8, 128),
        in_specs=[smem] + [vmem] * 7,
        out_specs=vmem,
        compiler_params=params(),
    )(decay, edge, u, s1, va, cax, crad, caz)


def azim_odd():
    return lax.rem(lax.axis_index("azim"), 2) == 1


def edges_kernel(scale, known, inlet, own_low, own_high, below, above, *refs):
    given, low, high = refs[:-2], refs[-2], refs[-1]
    factors = given[0]
    position = lax.axis_index("axial")
    fields = inlet.shape[0]
    if not known:
        a0, a3 = own_low[fields], own_high[fields]
        a_below = jnp.where(position == 0, a0, below[fields])
        a_above = above[fields]
        is_last = position == lax.axis_size("axial") - 1
        m_low = jnp.maximum(jnp.abs(a0), jnp.abs(a_below))
        m_up = jnp.maximum(jnp.abs(a3), jnp.abs(a_above))
        factors[0] = -12.0 * m_low
        factors[1] = 12.0 * (m_low + a_below)
        factors[2] = jnp.where(is_last, -12.0 * a3, -12.0 * m_up)
        factors[3] = jnp.where(is_last, 0.0, 12.0 * (m_up - a_above))
    for f in range(fields):
        from_below = jnp.where(position == 0, inlet[f], below[f])
        low[f] = scale * (factors[0] * own_low[f] + factors[1] * from_below)
        high[f] = scale * (factors[2] * own_high[f] + factors[3] * above[f])


def edges(scale, inlet, own_low, own_high, below, above, factors=None):
    fields = inlet.shape[0]
    known = factors is not None
    given = [inlet, own_low, own_high, below, above] + ([factors] if known else [])
    out = [arr(fields, 16, 128)] * 2
    if not known:
        out = [arr(4, 16, 128)] + out
    result = pl.pallas_call(
        functools.partial(edges_kernel, scale, known),
        out_shape=out,
        in_specs=[vmem] * len(given),
        out_specs=[vmem] * len(out),
        compiler_params=params(),
    )(*given)
    return ([factors] if known else []) + list(result)


def close_kernel(
    low, high, below, above, u, va, acc, s1, cross, chip, rows_low, rows_high, caz
):
    fields = u.shape[0]
    sub = lax.broadcasted_iota(jnp.int32, tile, 0)
    odd = azim_odd()
    for recv, plane, beside, sign in ((below, 0, 1, 1.0), (above, 3, 2, -1.0)):
        for k in range(16):
            own, other = va[0, plane, k], recv[fields, k]
            m = jnp.maximum(jnp.abs(own), jnp.abs(other))
            caz[plane, k] = -12.0 * m
            caz[beside, k] = 12.0 * (m + sign * other)

    def field(f, carry):
        def row(k, first, last):
            rows_low[f, k : k + 1, :] = first
            rows_high[f, k : k + 1, :] = last

        faces = []
        for recv, plane, beside in ((below, 0, 1), (above, 3, 2)):
            values = []
            for k in range(16):
                value = acc[f, plane, k] + (
                    caz[plane, k] * u[f, plane, k] + caz[beside, k] * recv[f, k]
                )
                if k < 4:
                    term = low[f, pl.ds(plane * 4 + k, 1), :]
                    value += jnp.where(sub == 0, term, 0.0)
                if k >= 12:
                    term = high[f, pl.ds(plane * 4 + k - 12, 1), :]
                    value += jnp.where(sub == 7, term, 0.0)
                values.append(value)
            for k in range(16):
                s1[f, plane, k] = values[k]
            for r in range(4):
                row(plane * 4 + r, values[r][0:1], values[12 + r][7:8])
            faces.append(values)
        for k in range(16):
            cross[f, k] = jnp.where(odd, faces[1][k], faces[0][k])
            chip[f, k] = jnp.where(odd, faces[0][k], faces[1][k])
        for a in (1, 2):
            for r in range(4):
                k = a * 4 + r
                first = acc[f, a, r, 0:1, :] + low[f, k : k + 1, :]
                last = acc[f, a, 12 + r, 7:8, :] + high[f, k : k + 1, :]
                s1[f, a, r, 0:1, :] = first
                s1[f, a, 12 + r, 7:8, :] = last
                row(k, first, last)
        return carry

    lax.fori_loop(0, fields, field, 0)


def close_first(low, high, below, above, u, va, acc):
    fields = u.shape[0]
    return pl.pallas_call(
        close_kernel,
        out_shape=[
            arr(fields, 4, 16, 8, 128),
            arr(fields, 16, 8, 128),
            arr(fields, 16, 8, 128),
            arr(fields, 16, 128),
            arr(fields, 16, 128),
            arr(4, 16, 8, 128),
        ],
        in_specs=[vmem] * 7,
        out_specs=[vmem] * 6,
        input_output_aliases={6: 0},
        compiler_params=params(),
    )(low, high, below, above, u, va, acc)


def finish_kernel(
    low, high, cross, chip, caz, part, out, work, sems
):
    fields = part.shape[0]
    sub = lax.broadcasted_iota(jnp.int32, tile, 0)
    odd = azim_odd()

    def field(f, carry):
        def edged(a, k, value):
            if k < 4:
                row = low[f, pl.ds(a * 4 + k, 1), :]
                return value + jnp.where(sub == 0, row, 0.0)
            if k >= 12:
                row = high[f, pl.ds(a * 4 + k - 12, 1), :]
                return value + jnp.where(sub == 7, row, 0.0)
            return value

        for lower, upper, plane, beside in ((cross, chip, 0, 1), (chip, cross, 3, 2)):
            values = []
            for k in range(16):
                received = jnp.where(odd, upper[f, k], lower[f, k])
                value = part[f, plane, k] + 0.5 * (caz[beside, k] * received)
                values.append(edged(plane, k, value))
            for k in range(16):
                work[f, plane, k] = values[k]
        for a in (1, 2):
            values = [edged(a, k, part[f, a, k]) for k in range(16)]
            for k in range(16):
                work[f, a, k] = values[k]
        pltpu.make_async_copy(work.at[f], out.at[f], sems.at[f]).start()
        return carry

    lax.fori_loop(0, fields, field, 0)

    def drain(f, carry):
        pltpu.make_async_copy(work.at[f], out.at[f], sems.at[f]).wait()
        return carry

    lax.fori_loop(0, fields, drain, 0)


def finish(low, high, cross, chip, caz, part):
    fields = part.shape[0]
    return pl.pallas_call(
        finish_kernel,
        out_shape=arr(*part.shape),
        in_specs=[vmem] * 6,
        out_specs=in_hbm,
        scratch_shapes=[
            pltpu.VMEM(part.shape, jnp.float32),
            pltpu.SemaphoreType.DMA((fields,)),
        ],
        compiler_params=params(),
    )(low, high, cross, chip, caz, part)


def exchange(low, high, axis):
    count = lax.axis_size(axis)
    up = [(i, (i + 1) % count) for i in range(count)]
    down = [(j, i) for i, j in up]
    return lax.ppermute(high, axis, up), lax.ppermute(low, axis, down)


def pair(array, axis, crossing):
    count = lax.axis_size(axis)
    step = 1 if crossing else -1
    route = [(i, (i + step) % count if i % 2 else (i - step) % count) for i in range(count)]
    return lax.ppermute(array, axis, route)


def per_device(flow_state, velocity, inlet_state, radial_inflow, face_tags, decay_rates):
    fields = flow_state.shape[0]
    u = flow_state.reshape((fields, 4, 16) + tile)
    vel = velocity.reshape((3, 4, 16) + tile)
    inlet = inlet_state.reshape(fields, 16, 128)
    lane = lax.broadcasted_iota(jnp.int32, tile, 1)
    tags = jnp.where(lane == 0, face_tags[0].reshape(8, 1), face_tags[1].reshape(8, 1))
    inflow = radial_inflow.transpose(0, 2, 3, 4, 5, 1).reshape(2, 16, 8, fields)

    rows_low, rows_high, face_low, face_high = depart(u, vel)
    row_below, row_above = exchange(rows_low, rows_high, "axial")
    below, above = exchange(face_low, face_high, "azim")

    va, cax, crad, edge = prepare(tags, inflow, vel)
    acc = first_section(decay_rates, edge, u, va, cax, crad)
    factors, low, high = edges(1.0, inlet, rows_low, rows_high, row_below, row_above)
    s1, cross, chip, rows_low, rows_high, caz = close_first(
        low, high, below, above, u, va, acc
    )
    row_below, row_above = exchange(rows_low, rows_high, "axial")
    cross, chip = pair(cross, "azim", True), pair(chip, "azim", False)

    part = second_section(decay_rates, edge, u, s1, va, cax, crad, caz)
    _, low, high = edges(0.5, inlet, rows_low, rows_high, row_below, row_above, factors)
    out = finish(low, high, cross, chip, caz, part)
    return out.reshape(flow_state.shape)


def solution(mesh):
    in_specs = (
        P(None, None, None, None, "azim", "axial", None),
        P(None, None, None, None, "azim", "axial", None),
        P(None, None, None, "azim", None),
        P(None, None, None, None, "azim", "axial"),
        P(None, "azim", "axial"),
        P(),
    )
    out_specs = P(None, None, None, None, "azim", "axial", None)
    return jax.shard_map(
        per_device, mesh=mesh, in_specs=in_specs, out_specs=out_specs, check_vma=False
    )
```

```python
import functools

import jax
import jax.numpy as jnp
import numpy as np
from jax import lax
from jax.experimental import pallas as pl
from jax.experimental.pallas import tpu as pltpu
from jax.sharding import PartitionSpec as P

time_step = 0.025
metric_scales = (2.0, 1.6, 2.4)
root5 = float(np.sqrt(5.0))
speed_scales = tuple(0.25 * c * time_step for c in metric_scales)
vmem = pl.BlockSpec(memory_space=pltpu.VMEM)
smem = pl.BlockSpec(memory_space=pltpu.SMEM)
anywhere = pl.BlockSpec(memory_space=pl.ANY)
in_hbm = pl.BlockSpec(memory_space=pltpu.HBM)
vmem_limit = 16 * 1024 * 1024
tile = (8, 128)


def params(limit=vmem_limit):
    return pltpu.CompilerParams(vmem_limit_bytes=limit)


def arr(*shape):
    return jax.ShapeDtypeStruct(shape, jnp.float32)


def volume(g0, g1, g2, g3):
    e0, o0, e1, o1 = g0 + g3, g0 - g3, g1 + g2, g1 - g2
    h1 = root5 * o1
    s03 = o0 - 5.0 * h1
    d03 = e0 + 5.0 * e1
    s12 = o0 + h1
    d12 = root5 * (e0 - e1)
    return s03 - d03, s12 + d12, s12 - d12, s03 + d03


def depart_kernel(u, vel, rows_low, rows_high, face_low, face_high):
    fields = u.shape[0]

    def put(f, a, low, high):
        for r in range(4):
            k = a * 4 + r
            rows_low[f, k : k + 1, :] = low[r]
            rows_high[f, k : k + 1, :] = high[r]

    def field(f, carry):
        for a in range(4):
            put(
                f,
                a,
                [u[f, a, r, 0:1, :] for r in range(4)],
                [u[f, a, 12 + r, 7:8, :] for r in range(4)],
            )
        for dst, plane in ((face_low, 0), (face_high, 3)):
            values = [u[f, plane, k] for k in range(16)]
            for k in range(16):
                dst[f, k] = values[k]
        return carry

    lax.fori_loop(0, fields, field, 0)
    for a in range(4):
        put(
            fields,
            a,
            [vel[1, a, r, 0:1, :] * speed_scales[1] for r in range(4)],
            [vel[1, a, 12 + r, 7:8, :] * speed_scales[1] for r in range(4)],
        )
    for dst, plane in ((face_low, 0), (face_high, 3)):
        values = [vel[0, plane, k] * speed_scales[0] for k in range(16)]
        for k in range(16):
            dst[fields, k] = values[k]


def depart(u, vel):
    fields = u.shape[0]
    return pl.pallas_call(
        depart_kernel,
        out_shape=[arr(fields + 1, 16, 128)] * 2 + [arr(fields + 1, 16, 8, 128)] * 2,
        in_specs=[vmem] * 2,
        out_specs=[vmem] * 4,
        compiler_params=params(),
    )(u, vel)


def prepare_kernel(tags, inflow, vel, va, cax, crad, edge):
    lane = lax.broadcasted_iota(jnp.int32, tile, 1)
    sub = lax.broadcasted_iota(jnp.int32, tile, 0)
    tag = tags[...]
    inner, outer = lane == 0, lane == 127

    def imposed(k, carry):
        within, beyond = inflow[0, k], inflow[1, k]
        for f in range(edge.shape[0]):
            edge[f, k] = jnp.where(inner, within[:, f : f + 1], beyond[:, f : f + 1])
        return carry

    lax.fori_loop(0, 16, imposed, 0)

    def plane(a, carry):
        for d in range(3):
            for k in range(16):
                va[d, a, k] = vel[d, a, k] * speed_scales[d]
        for r in range(4):
            a0, a3 = va[1, a, r], va[1, a, 12 + r]
            below, above = pltpu.roll(a3, 1, 0), pltpu.roll(a0, 7, 0)
            m_low = jnp.maximum(jnp.abs(a0), jnp.abs(below))
            m_up = jnp.maximum(jnp.abs(a3), jnp.abs(above))
            cax[a, r, 0] = jnp.where(sub == 0, 0.0, -12.0 * m_low)
            cax[a, r, 1] = jnp.where(sub == 0, 0.0, 12.0 * (m_low + below))
            cax[a, r, 2] = jnp.where(sub == 7, 0.0, -12.0 * m_up)
            cax[a, r, 3] = jnp.where(sub == 7, 0.0, 12.0 * (m_up - above))
        for x in range(4):
            a0, a3 = va[2, a, 4 * x], va[2, a, 4 * x + 3]
            below = jnp.where(inner, a0, pltpu.roll(a3, 1, 1))
            above = jnp.where(outer, a3, pltpu.roll(a0, 127, 1))
            m_low = jnp.maximum(jnp.abs(a0), jnp.abs(below))
            m_up = jnp.maximum(jnp.abs(a3), jnp.abs(above))
            own_low, out_low = -12.0 * m_low, 12.0 * (m_low + below)
            own_up, out_up = -12.0 * m_up, 12.0 * (m_up - above)
            own_low = jnp.where(inner & (tag == 0), -12.0 * a0, own_low)
            own_low = jnp.where(inner & (tag == 2), 12.0 * a0, own_low)
            own_up = jnp.where(outer & (tag == 0), 12.0 * a3, own_up)
            own_up = jnp.where(outer & (tag == 2), -12.0 * a3, own_up)
            crad[a, x, 0] = own_low
            crad[a, x, 1] = jnp.where(inner & (tag != 1), 0.0, out_low)
            crad[a, x, 2] = own_up
            crad[a, x, 3] = jnp.where(outer & (tag != 1), 0.0, out_up)
        return carry

    lax.fori_loop(0, 4, plane, 0)


def prepare(tags, inflow, vel):
    return pl.pallas_call(
        prepare_kernel,
        out_shape=[
            arr(3, 4, 16, 8, 128),
            arr(4, 4, 4, 8, 128),
            arr(4, 4, 4, 8, 128),
            arr(inflow.shape[-1], 16, 8, 128),
        ],
        in_specs=[vmem] * 3,
        out_specs=[vmem] * 4,
        compiler_params=params(),
    )(tags, inflow, vel)


def plane_terms(f, a, keep, src, va, cax, crad, edge):
    lane = lax.broadcasted_iota(jnp.int32, tile, 1)
    u = [src[f, a, k] for k in range(16)]
    acc = [keep * v for v in u]
    for r in range(4):
        line = [u[4 * x + r] for x in range(4)]
        out = volume(*[va[1, a, 4 * x + r] * line[x] for x in range(4)])
        below, above = pltpu.roll(line[3], 1, 0), pltpu.roll(line[0], 7, 0)
        acc[r] += out[0] + (cax[a, r, 0] * line[0] + cax[a, r, 1] * below)
        acc[4 + r] += out[1]
        acc[8 + r] += out[2]
        acc[12 + r] += out[3] + (cax[a, r, 2] * line[3] + cax[a, r, 3] * above)
    for x in range(4):
        line = [u[4 * x + r] for r in range(4)]
        out = volume(*[va[2, a, 4 * x + r] * line[r] for r in range(4)])
        imposed = edge[f, a * 4 + x]
        below = jnp.where(lane == 0, imposed, pltpu.roll(line[3], 1, 1))
        above = jnp.where(lane == 127, imposed, pltpu.roll(line[0], 127, 1))
        acc[4 * x] += out[0] + (crad[a, x, 0] * line[0] + crad[a, x, 1] * below)
        acc[4 * x + 1] += out[1]
        acc[4 * x + 2] += out[2]
        acc[4 * x + 3] += out[3] + (crad[a, x, 2] * line[3] + crad[a, x, 3] * above)
    return acc


def first_kernel(decay, edge, u, va, cax, crad, acc):
    fields = u.shape[0]

    def field(f, carry):
        keep = 1.0 - time_step * decay[f]
        for q in range(4):
            outs = []
            for k in range(4 * q, 4 * q + 4):
                outs.append(volume(*[va[0, a, k] * u[f, a, k] for a in range(4)]))
            for r in range(4):
                for a in range(4):
                    acc[f, a, 4 * q + r] = outs[r][a]
        for a in range(4):
            out = plane_terms(f, a, keep, u, va, cax, crad, edge)
            for k in range(16):
                acc[f, a, k] += out[k]
        return carry

    lax.fori_loop(0, fields, field, 0)


def first_section(decay, edge, u, va, cax, crad):
    fields = u.shape[0]
    return pl.pallas_call(
        first_kernel,
        out_shape=arr(fields, 4, 16, 8, 128),
        in_specs=[smem] + [vmem] * 5,
        out_specs=vmem,
        compiler_params=params(),
    )(decay, edge, u, va, cax, crad)


def second_kernel(decay, edge, u, s1, va, cax, crad, caz, part):
    fields = u.shape[0]

    def field(f, carry):
        keep = 1.0 - time_step * decay[f]
        for q in range(4):
            outs = []
            for k in range(4 * q, 4 * q + 4):
                line = [s1[f, a, k] for a in range(4)]
                out = list(volume(*[va[0, a, k] * line[a] for a in range(4)]))
                out[0] += caz[0, k] * line[0]
                out[3] += caz[3, k] * line[3]
                outs.append(out)
            for r in range(4):
                for a in range(4):
                    part[f, a, 4 * q + r] = outs[r][a]
        for a in range(4):
            out = plane_terms(f, a, keep, s1, va, cax, crad, edge)
            for k in range(16):
                part[f, a, k] = 0.5 * (u[f, a, k] + (part[f, a, k] + out[k]))
        return carry

    lax.fori_loop(0, fields, field, 0)


def second_section(decay, edge, u, s1, va, cax, crad, caz):
    fields = u.shape[0]
    return pl.pallas_call(
        second_kernel,
        out_shape=arr(fields, 4, 16, 8, 128),
        in_specs=[smem] + [vmem] * 7,
        out_specs=vmem,
        compiler_params=params(),
    )(decay, edge, u, s1, va, cax, crad, caz)


def azim_odd():
    return lax.rem(lax.axis_index("azim"), 2) == 1


def edges_kernel(scale, known, inlet, own_low, own_high, below, above, *refs):
    given, low, high = refs[:-2], refs[-2], refs[-1]
    factors = given[0]
    position = lax.axis_index("axial")
    fields = inlet.shape[0]
    if not known:
        a0, a3 = own_low[fields], own_high[fields]
        a_below = jnp.where(position == 0, a0, below[fields])
        a_above = above[fields]
        is_last = position == lax.axis_size("axial") - 1
        m_low = jnp.maximum(jnp.abs(a0), jnp.abs(a_below))
        m_up = jnp.maximum(jnp.abs(a3), jnp.abs(a_above))
        factors[0] = -12.0 * m_low
        factors[1] = 12.0 * (m_low + a_below)
        factors[2] = jnp.where(is_last, -12.0 * a3, -12.0 * m_up)
        factors[3] = jnp.where(is_last, 0.0, 12.0 * (m_up - a_above))
    for f in range(fields):
        from_below = jnp.where(position == 0, inlet[f], below[f])
        low[f] = scale * (factors[0] * own_low[f] + factors[1] * from_below)
        high[f] = scale * (factors[2] * own_high[f] + factors[3] * above[f])


def edges(scale, inlet, own_low, own_high, below, above, factors=None):
    fields = inlet.shape[0]
    known = factors is not None
    given = [inlet, own_low, own_high, below, above] + ([factors] if known else [])
    out = [arr(fields, 16, 128)] * 2
    if not known:
        out = [arr(4, 16, 128)] + out
    result = pl.pallas_call(
        functools.partial(edges_kernel, scale, known),
        out_shape=out,
        in_specs=[vmem] * len(given),
        out_specs=[vmem] * len(out),
        compiler_params=params(),
    )(*given)
    return ([factors] if known else []) + list(result)


def close_kernel(
    low, high, below, above, u, va, acc, s1, cross, chip, rows_low, rows_high, caz
):
    fields = u.shape[0]
    sub = lax.broadcasted_iota(jnp.int32, tile, 0)
    odd = azim_odd()
    for recv, plane, beside, sign in ((below, 0, 1, 1.0), (above, 3, 2, -1.0)):
        for k in range(16):
            own, other = va[0, plane, k], recv[fields, k]
            m = jnp.maximum(jnp.abs(own), jnp.abs(other))
            caz[plane, k] = -12.0 * m
            caz[beside, k] = 12.0 * (m + sign * other)

    def field(f, carry):
        def row(k, first, last):
            rows_low[f, k : k + 1, :] = first
            rows_high[f, k : k + 1, :] = last

        faces = []
        for recv, plane, beside in ((below, 0, 1), (above, 3, 2)):
            values = []
            for k in range(16):
                value = acc[f, plane, k] + (
                    caz[plane, k] * u[f, plane, k] + caz[beside, k] * recv[f, k]
                )
                if k < 4:
                    term = low[f, pl.ds(plane * 4 + k, 1), :]
                    value += jnp.where(sub == 0, term, 0.0)
                if k >= 12:
                    term = high[f, pl.ds(plane * 4 + k - 12, 1), :]
                    value += jnp.where(sub == 7, term, 0.0)
                values.append(value)
            for k in range(16):
                s1[f, plane, k] = values[k]
            for r in range(4):
                row(plane * 4 + r, values[r][0:1], values[12 + r][7:8])
            faces.append(values)
        for k in range(16):
            cross[f, k] = jnp.where(odd, faces[1][k], faces[0][k])
            chip[f, k] = jnp.where(odd, faces[0][k], faces[1][k])
        for a in (1, 2):
            for r in range(4):
                k = a * 4 + r
                first = acc[f, a, r, 0:1, :] + low[f, k : k + 1, :]
                last = acc[f, a, 12 + r, 7:8, :] + high[f, k : k + 1, :]
                s1[f, a, r, 0:1, :] = first
                s1[f, a, 12 + r, 7:8, :] = last
                row(k, first, last)
        return carry

    lax.fori_loop(0, fields, field, 0)


def close_first(low, high, below, above, u, va, acc):
    fields = u.shape[0]
    return pl.pallas_call(
        close_kernel,
        out_shape=[
            arr(fields, 4, 16, 8, 128),
            arr(fields, 16, 8, 128),
            arr(fields, 16, 8, 128),
            arr(fields, 16, 128),
            arr(fields, 16, 128),
            arr(4, 16, 8, 128),
        ],
        in_specs=[vmem] * 7,
        out_specs=[vmem] * 6,
        input_output_aliases={6: 0},
        compiler_params=params(),
    )(low, high, below, above, u, va, acc)


def finish_kernel(
    low, high, chip, cross, caz, part, out, work, sems
):
    fields = part.shape[0]
    sub = lax.broadcasted_iota(jnp.int32, tile, 0)
    odd = azim_odd()

    def field(f, carry):
        def edged(a, k, value):
            if k < 4:
                row = low[f, pl.ds(a * 4 + k, 1), :]
                return value + jnp.where(sub == 0, row, 0.0)
            if k >= 12:
                row = high[f, pl.ds(a * 4 + k - 12, 1), :]
                return value + jnp.where(sub == 7, row, 0.0)
            return value

        for lower, upper, plane, beside in ((cross, chip, 0, 1), (chip, cross, 3, 2)):
            values = []
            for k in range(16):
                received = jnp.where(odd, upper[f, k], lower[f, k])
                value = part[f, plane, k] + 0.5 * (caz[beside, k] * received)
                values.append(edged(plane, k, value))
            for k in range(16):
                work[f, plane, k] = values[k]
        for a in (1, 2):
            values = [edged(a, k, part[f, a, k]) for k in range(16)]
            for k in range(16):
                work[f, a, k] = values[k]
        pltpu.make_async_copy(work.at[f], out.at[f], sems.at[f]).start()
        return carry

    lax.fori_loop(0, fields, field, 0)

    def drain(f, carry):
        pltpu.make_async_copy(work.at[f], out.at[f], sems.at[f]).wait()
        return carry

    lax.fori_loop(0, fields, drain, 0)


def finish(low, high, chip, cross, caz, part):
    fields = part.shape[0]
    return pl.pallas_call(
        finish_kernel,
        out_shape=arr(*part.shape),
        in_specs=[vmem] * 6,
        out_specs=in_hbm,
        scratch_shapes=[
            pltpu.VMEM(part.shape, jnp.float32),
            pltpu.SemaphoreType.DMA((fields,)),
        ],
        compiler_params=params(),
    )(low, high, chip, cross, caz, part)


def exchange(low, high, axis):
    count = lax.axis_size(axis)
    up = [(i, (i + 1) % count) for i in range(count)]
    down = [(j, i) for i, j in up]
    return lax.ppermute(high, axis, up), lax.ppermute(low, axis, down)


def pair(array, axis, crossing):
    count = lax.axis_size(axis)
    step = 1 if crossing else -1
    route = [(i, (i + step) % count if i % 2 else (i - step) % count) for i in range(count)]
    return lax.ppermute(array, axis, route)


def per_device(flow_state, velocity, inlet_state, radial_inflow, face_tags, decay_rates):
    fields = flow_state.shape[0]
    u = flow_state.reshape((fields, 4, 16) + tile)
    vel = velocity.reshape((3, 4, 16) + tile)
    inlet = inlet_state.reshape(fields, 16, 128)
    lane = lax.broadcasted_iota(jnp.int32, tile, 1)
    tags = jnp.where(lane == 0, face_tags[0].reshape(8, 1), face_tags[1].reshape(8, 1))
    inflow = radial_inflow.transpose(0, 2, 3, 4, 5, 1).reshape(2, 16, 8, fields)

    rows_low, rows_high, face_low, face_high = depart(u, vel)
    row_below, row_above = exchange(rows_low, rows_high, "axial")
    below, above = exchange(face_low, face_high, "azim")

    va, cax, crad, edge = prepare(tags, inflow, vel)
    acc = first_section(decay_rates, edge, u, va, cax, crad)
    factors, low, high = edges(1.0, inlet, rows_low, rows_high, row_below, row_above)
    s1, cross, chip, rows_low, rows_high, caz = close_first(
        low, high, below, above, u, va, acc
    )
    row_below, row_above = exchange(rows_low, rows_high, "axial")
    chip, cross = pair(chip, "azim", False), pair(cross, "azim", True)

    part = second_section(decay_rates, edge, u, s1, va, cax, crad, caz)
    _, low, high = edges(0.5, inlet, rows_low, rows_high, row_below, row_above, factors)
    out = finish(low, high, chip, cross, caz, part)
    return out.reshape(flow_state.shape)


def solution(mesh):
    in_specs = (
        P(None, None, None, None, "azim", "axial", None),
        P(None, None, None, None, "azim", "axial", None),
        P(None, None, None, "azim", None),
        P(None, None, None, None, "azim", "axial"),
        P(None, "azim", "axial"),
        P(),
    )
    out_specs = P(None, None, None, None, "azim", "axial", None)
    return jax.shard_map(
        per_device, mesh=mesh, in_specs=in_specs, out_specs=out_specs, check_vma=False
    )
```

```python
import functools

import jax
import jax.numpy as jnp
import numpy as np
from jax import lax
from jax.experimental import pallas as pl
from jax.experimental.pallas import tpu as pltpu
from jax.sharding import PartitionSpec as P

time_step = 0.025
metric_scales = (2.0, 1.6, 2.4)
root5 = float(np.sqrt(5.0))
speed_scales = tuple(0.25 * c * time_step for c in metric_scales)
vmem = pl.BlockSpec(memory_space=pltpu.VMEM)
smem = pl.BlockSpec(memory_space=pltpu.SMEM)
anywhere = pl.BlockSpec(memory_space=pl.ANY)
in_hbm = pl.BlockSpec(memory_space=pltpu.HBM)
vmem_limit = 16 * 1024 * 1024
tile = (8, 128)


def params(limit=vmem_limit):
    return pltpu.CompilerParams(vmem_limit_bytes=limit)


def arr(*shape):
    return jax.ShapeDtypeStruct(shape, jnp.float32)


def volume(g0, g1, g2, g3):
    e0, o0, e1, o1 = g0 + g3, g0 - g3, g1 + g2, g1 - g2
    h1 = root5 * o1
    s03 = o0 - 5.0 * h1
    d03 = e0 + 5.0 * e1
    s12 = o0 + h1
    d12 = root5 * (e0 - e1)
    return s03 - d03, s12 + d12, s12 - d12, s03 + d03


def depart_kernel(u, vel, rows_low, rows_high, face_low, face_high):
    fields = u.shape[0]

    def put(f, a, low, high):
        for r in range(4):
            k = a * 4 + r
            rows_low[f, k : k + 1, :] = low[r]
            rows_high[f, k : k + 1, :] = high[r]

    def field(f, carry):
        for a in range(4):
            put(
                f,
                a,
                [u[f, a, r, 0:1, :] for r in range(4)],
                [u[f, a, 12 + r, 7:8, :] for r in range(4)],
            )
        for dst, plane in ((face_low, 0), (face_high, 3)):
            values = [u[f, plane, k] for k in range(16)]
            for k in range(16):
                dst[f, k] = values[k]
        return carry

    lax.fori_loop(0, fields, field, 0)
    for a in range(4):
        put(
            fields,
            a,
            [vel[1, a, r, 0:1, :] * speed_scales[1] for r in range(4)],
            [vel[1, a, 12 + r, 7:8, :] * speed_scales[1] for r in range(4)],
        )
    for dst, plane in ((face_low, 0), (face_high, 3)):
        values = [vel[0, plane, k] * speed_scales[0] for k in range(16)]
        for k in range(16):
            dst[fields, k] = values[k]


def depart(u, vel):
    fields = u.shape[0]
    return pl.pallas_call(
        depart_kernel,
        out_shape=[arr(fields + 1, 16, 128)] * 2 + [arr(fields + 1, 16, 8, 128)] * 2,
        in_specs=[vmem] * 2,
        out_specs=[vmem] * 4,
        compiler_params=params(),
    )(u, vel)


def prepare_kernel(tags, inflow, vel, va, cax, crad, edge):
    lane = lax.broadcasted_iota(jnp.int32, tile, 1)
    sub = lax.broadcasted_iota(jnp.int32, tile, 0)
    tag = tags[...]
    inner, outer = lane == 0, lane == 127

    def imposed(k, carry):
        within, beyond = inflow[0, k], inflow[1, k]
        for f in range(edge.shape[0]):
            edge[f, k] = jnp.where(inner, within[:, f : f + 1], beyond[:, f : f + 1])
        return carry

    lax.fori_loop(0, 16, imposed, 0)

    def plane(a, carry):
        for d in range(3):
            for k in range(16):
                va[d, a, k] = vel[d, a, k] * speed_scales[d]
        for r in range(4):
            a0, a3 = va[1, a, r], va[1, a, 12 + r]
            below, above = pltpu.roll(a3, 1, 0), pltpu.roll(a0, 7, 0)
            m_low = jnp.maximum(jnp.abs(a0), jnp.abs(below))
            m_up = jnp.maximum(jnp.abs(a3), jnp.abs(above))
            cax[a, r, 0] = jnp.where(sub == 0, 0.0, -12.0 * m_low)
            cax[a, r, 1] = jnp.where(sub == 0, 0.0, 12.0 * (m_low + below))
            cax[a, r, 2] = jnp.where(sub == 7, 0.0, -12.0 * m_up)
            cax[a, r, 3] = jnp.where(sub == 7, 0.0, 12.0 * (m_up - above))
        for x in range(4):
            a0, a3 = va[2, a, 4 * x], va[2, a, 4 * x + 3]
            below = jnp.where(inner, a0, pltpu.roll(a3, 1, 1))
            above = jnp.where(outer, a3, pltpu.roll(a0, 127, 1))
            m_low = jnp.maximum(jnp.abs(a0), jnp.abs(below))
            m_up = jnp.maximum(jnp.abs(a3), jnp.abs(above))
            own_low, out_low = -12.0 * m_low, 12.0 * (m_low + below)
            own_up, out_up = -12.0 * m_up, 12.0 * (m_up - above)
            own_low = jnp.where(inner & (tag == 0), -12.0 * a0, own_low)
            own_low = jnp.where(inner & (tag == 2), 12.0 * a0, own_low)
            own_up = jnp.where(outer & (tag == 0), 12.0 * a3, own_up)
            own_up = jnp.where(outer & (tag == 2), -12.0 * a3, own_up)
            crad[a, x, 0] = own_low
            crad[a, x, 1] = jnp.where(inner & (tag != 1), 0.0, out_low)
            crad[a, x, 2] = own_up
            crad[a, x, 3] = jnp.where(outer & (tag != 1), 0.0, out_up)
        return carry

    lax.fori_loop(0, 4, plane, 0)


def prepare(tags, inflow, vel):
    return pl.pallas_call(
        prepare_kernel,
        out_shape=[
            arr(3, 4, 16, 8, 128),
            arr(4, 4, 4, 8, 128),
            arr(4, 4, 4, 8, 128),
            arr(inflow.shape[-1], 16, 8, 128),
        ],
        in_specs=[vmem] * 3,
        out_specs=[vmem] * 4,
        compiler_params=params(),
    )(tags, inflow, vel)


def plane_terms(f, a, keep, src, va, cax, crad, edge):
    lane = lax.broadcasted_iota(jnp.int32, tile, 1)
    u = [src[f, a, k] for k in range(16)]
    acc = [keep * v for v in u]
    for r in range(4):
        line = [u[4 * x + r] for x in range(4)]
        out = volume(*[va[1, a, 4 * x + r] * line[x] for x in range(4)])
        below, above = pltpu.roll(line[3], 1, 0), pltpu.roll(line[0], 7, 0)
        acc[r] += out[0] + (cax[a, r, 0] * line[0] + cax[a, r, 1] * below)
        acc[4 + r] += out[1]
        acc[8 + r] += out[2]
        acc[12 + r] += out[3] + (cax[a, r, 2] * line[3] + cax[a, r, 3] * above)
    for x in range(4):
        line = [u[4 * x + r] for r in range(4)]
        out = volume(*[va[2, a, 4 * x + r] * line[r] for r in range(4)])
        imposed = edge[f, a * 4 + x]
        below = jnp.where(lane == 0, imposed, pltpu.roll(line[3], 1, 1))
        above = jnp.where(lane == 127, imposed, pltpu.roll(line[0], 127, 1))
        acc[4 * x] += out[0] + (crad[a, x, 0] * line[0] + crad[a, x, 1] * below)
        acc[4 * x + 1] += out[1]
        acc[4 * x + 2] += out[2]
        acc[4 * x + 3] += out[3] + (crad[a, x, 2] * line[3] + crad[a, x, 3] * above)
    return acc


def first_kernel(decay, edge, u, va, cax, crad, acc):
    fields = u.shape[0]

    def field(f, carry):
        keep = 1.0 - time_step * decay[f]
        for q in range(4):
            outs = []
            for k in range(4 * q, 4 * q + 4):
                outs.append(volume(*[va[0, a, k] * u[f, a, k] for a in range(4)]))
            for r in range(4):
                for a in range(4):
                    acc[f, a, 4 * q + r] = outs[r][a]
        for a in range(4):
            out = plane_terms(f, a, keep, u, va, cax, crad, edge)
            for k in range(16):
                acc[f, a, k] += out[k]
        return carry

    lax.fori_loop(0, fields, field, 0)


def first_section(decay, edge, u, va, cax, crad):
    fields = u.shape[0]
    return pl.pallas_call(
        first_kernel,
        out_shape=arr(fields, 4, 16, 8, 128),
        in_specs=[smem] + [vmem] * 5,
        out_specs=vmem,
        compiler_params=params(),
    )(decay, edge, u, va, cax, crad)


def second_kernel(decay, edge, u, s1, va, cax, crad, caz, part):
    fields = u.shape[0]

    def field(f, carry):
        keep = 1.0 - time_step * decay[f]
        for q in range(4):
            outs = []
            for k in range(4 * q, 4 * q + 4):
                line = [s1[f, a, k] for a in range(4)]
                out = list(volume(*[va[0, a, k] * line[a] for a in range(4)]))
                out[0] += caz[0, k] * line[0]
                out[3] += caz[3, k] * line[3]
                outs.append(out)
            for r in range(4):
                for a in range(4):
                    part[f, a, 4 * q + r] = outs[r][a]
        for a in range(4):
            out = plane_terms(f, a, keep, s1, va, cax, crad, edge)
            for k in range(16):
                part[f, a, k] = 0.5 * (u[f, a, k] + (part[f, a, k] + out[k]))
        return carry

    lax.fori_loop(0, fields, field, 0)


def second_section(decay, edge, u, s1, va, cax, crad, caz):
    fields = u.shape[0]
    return pl.pallas_call(
        second_kernel,
        out_shape=arr(fields, 4, 16, 8, 128),
        in_specs=[smem] + [vmem] * 7,
        out_specs=vmem,
        compiler_params=params(),
    )(decay, edge, u, s1, va, cax, crad, caz)


def azim_odd():
    return lax.rem(lax.axis_index("azim"), 2) == 1


def edges_kernel(scale, known, inlet, own_low, own_high, below, above, *refs):
    given, low, high = refs[:-2], refs[-2], refs[-1]
    factors = given[0]
    position = lax.axis_index("axial")
    fields = inlet.shape[0]
    if not known:
        a0, a3 = own_low[fields], own_high[fields]
        a_below = jnp.where(position == 0, a0, below[fields])
        a_above = above[fields]
        is_last = position == lax.axis_size("axial") - 1
        m_low = jnp.maximum(jnp.abs(a0), jnp.abs(a_below))
        m_up = jnp.maximum(jnp.abs(a3), jnp.abs(a_above))
        factors[0] = -12.0 * m_low
        factors[1] = 12.0 * (m_low + a_below)
        factors[2] = jnp.where(is_last, -12.0 * a3, -12.0 * m_up)
        factors[3] = jnp.where(is_last, 0.0, 12.0 * (m_up - a_above))
    for f in range(fields):
        from_below = jnp.where(position == 0, inlet[f], below[f])
        low[f] = scale * (factors[0] * own_low[f] + factors[1] * from_below)
        high[f] = scale * (factors[2] * own_high[f] + factors[3] * above[f])


def edges(scale, inlet, own_low, own_high, below, above, factors=None):
    fields = inlet.shape[0]
    known = factors is not None
    given = [inlet, own_low, own_high, below, above] + ([factors] if known else [])
    out = [arr(fields, 16, 128)] * 2
    if not known:
        out = [arr(4, 16, 128)] + out
    result = pl.pallas_call(
        functools.partial(edges_kernel, scale, known),
        out_shape=out,
        in_specs=[vmem] * len(given),
        out_specs=[vmem] * len(out),
        compiler_params=params(),
    )(*given)
    return ([factors] if known else []) + list(result)


def close_kernel(
    low, high, below, above, u, va, acc, s1, cross, chip, rows_low, rows_high, caz
):
    fields = u.shape[0]
    sub = lax.broadcasted_iota(jnp.int32, tile, 0)
    odd = azim_odd()
    for recv, plane, beside, sign in ((below, 0, 1, 1.0), (above, 3, 2, -1.0)):
        for k in range(16):
            own, other = va[0, plane, k], recv[fields, k]
            m = jnp.maximum(jnp.abs(own), jnp.abs(other))
            caz[plane, k] = -12.0 * m
            caz[beside, k] = 12.0 * (m + sign * other)

    def field(f, carry):
        def row(k, first, last):
            rows_low[f, k : k + 1, :] = first
            rows_high[f, k : k + 1, :] = last

        faces = []
        for recv, plane, beside in ((below, 0, 1), (above, 3, 2)):
            values = []
            for k in range(16):
                value = acc[f, plane, k] + (
                    caz[plane, k] * u[f, plane, k] + caz[beside, k] * recv[f, k]
                )
                if k < 4:
                    term = low[f, pl.ds(plane * 4 + k, 1), :]
                    value += jnp.where(sub == 0, term, 0.0)
                if k >= 12:
                    term = high[f, pl.ds(plane * 4 + k - 12, 1), :]
                    value += jnp.where(sub == 7, term, 0.0)
                values.append(value)
            for k in range(16):
                s1[f, plane, k] = values[k]
            for r in range(4):
                row(plane * 4 + r, values[r][0:1], values[12 + r][7:8])
            faces.append(values)
        for k in range(16):
            cross[f, k] = jnp.where(odd, faces[1][k], faces[0][k])
            chip[f, k] = jnp.where(odd, faces[0][k], faces[1][k])
        for a in (1, 2):
            for r in range(4):
                k = a * 4 + r
                first = acc[f, a, r, 0:1, :] + low[f, k : k + 1, :]
                last = acc[f, a, 12 + r, 7:8, :] + high[f, k : k + 1, :]
                s1[f, a, r, 0:1, :] = first
                s1[f, a, 12 + r, 7:8, :] = last
                row(k, first, last)
        return carry

    lax.fori_loop(0, fields, field, 0)


def close_first(low, high, below, above, u, va, acc):
    fields = u.shape[0]
    return pl.pallas_call(
        close_kernel,
        out_shape=[
            arr(fields, 4, 16, 8, 128),
            arr(fields, 16, 8, 128),
            arr(fields, 16, 8, 128),
            arr(fields, 16, 128),
            arr(fields, 16, 128),
            arr(4, 16, 8, 128),
        ],
        in_specs=[vmem] * 7,
        out_specs=[vmem] * 6,
        input_output_aliases={6: 0},
        compiler_params=params(),
    )(low, high, below, above, u, va, acc)


def finish_kernel(
    low, high, chip, cross, caz, part, out, work, sems
):
    fields = part.shape[0]
    sub = lax.broadcasted_iota(jnp.int32, tile, 0)
    odd = azim_odd()

    def copy(src, f, planes, nodes, sem):
        at = (f, pl.ds(*planes), pl.ds(*nodes))
        return pltpu.make_async_copy(src.at[at], out.at[at], sems.at[f, sem])

    def early(f):
        return copy(part, f, (1, 2), (4, 8), 0)

    def late(f):
        return [
            copy(work, f, (0, 1), (0, 16), 1),
            copy(work, f, (3, 1), (0, 16), 2),
            copy(work, f, (1, 2), (0, 4), 3),
            copy(work, f, (1, 2), (12, 4), 4),
        ]

    def begin(f, carry):
        early(f).start()
        return carry

    lax.fori_loop(0, fields, begin, 0)

    def field(f, carry):
        def edged(a, k, value):
            if k < 4:
                row = low[f, pl.ds(a * 4 + k, 1), :]
                return value + jnp.where(sub == 0, row, 0.0)
            if k >= 12:
                row = high[f, pl.ds(a * 4 + k - 12, 1), :]
                return value + jnp.where(sub == 7, row, 0.0)
            return value

        for lower, upper, plane, beside in ((cross, chip, 0, 1), (chip, cross, 3, 2)):
            values = []
            for k in range(16):
                received = jnp.where(odd, upper[f, k], lower[f, k])
                value = part[f, plane, k] + 0.5 * (caz[beside, k] * received)
                values.append(edged(plane, k, value))
            for k in range(16):
                work[f, plane, k] = values[k]
        outer = (0, 1, 2, 3, 12, 13, 14, 15)
        for a in (1, 2):
            values = [edged(a, k, part[f, a, k]) for k in outer]
            for k, value in zip(outer, values):
                work[f, a, k] = value
        for c in late(f):
            c.start()
        return carry

    lax.fori_loop(0, fields, field, 0)

    def drain(f, carry):
        early(f).wait()
        for c in late(f):
            c.wait()
        return carry

    lax.fori_loop(0, fields, drain, 0)


def finish(low, high, chip, cross, caz, part):
    fields = part.shape[0]
    return pl.pallas_call(
        finish_kernel,
        out_shape=arr(*part.shape),
        in_specs=[vmem] * 6,
        out_specs=in_hbm,
        scratch_shapes=[
            pltpu.VMEM(part.shape, jnp.float32),
            pltpu.SemaphoreType.DMA((fields, 5)),
        ],
        compiler_params=params(),
    )(low, high, chip, cross, caz, part)


def exchange(low, high, axis):
    count = lax.axis_size(axis)
    up = [(i, (i + 1) % count) for i in range(count)]
    down = [(j, i) for i, j in up]
    return lax.ppermute(high, axis, up), lax.ppermute(low, axis, down)


def pair(array, axis, crossing):
    count = lax.axis_size(axis)
    step = 1 if crossing else -1
    route = [(i, (i + step) % count if i % 2 else (i - step) % count) for i in range(count)]
    return lax.ppermute(array, axis, route)


def per_device(flow_state, velocity, inlet_state, radial_inflow, face_tags, decay_rates):
    fields = flow_state.shape[0]
    u = flow_state.reshape((fields, 4, 16) + tile)
    vel = velocity.reshape((3, 4, 16) + tile)
    inlet = inlet_state.reshape(fields, 16, 128)
    lane = lax.broadcasted_iota(jnp.int32, tile, 1)
    tags = jnp.where(lane == 0, face_tags[0].reshape(8, 1), face_tags[1].reshape(8, 1))
    inflow = radial_inflow.transpose(0, 2, 3, 4, 5, 1).reshape(2, 16, 8, fields)

    rows_low, rows_high, face_low, face_high = depart(u, vel)
    row_below, row_above = exchange(rows_low, rows_high, "axial")
    below, above = exchange(face_low, face_high, "azim")

    va, cax, crad, edge = prepare(tags, inflow, vel)
    acc = first_section(decay_rates, edge, u, va, cax, crad)
    factors, low, high = edges(1.0, inlet, rows_low, rows_high, row_below, row_above)
    s1, cross, chip, rows_low, rows_high, caz = close_first(
        low, high, below, above, u, va, acc
    )
    row_below, row_above = exchange(rows_low, rows_high, "axial")
    chip, cross = pair(chip, "azim", False), pair(cross, "azim", True)

    part = second_section(decay_rates, edge, u, s1, va, cax, crad, caz)
    _, low, high = edges(0.5, inlet, rows_low, rows_high, row_below, row_above, factors)
    out = finish(low, high, chip, cross, caz, part)
    return out.reshape(flow_state.shape)


def solution(mesh):
    in_specs = (
        P(None, None, None, None, "azim", "axial", None),
        P(None, None, None, None, "azim", "axial", None),
        P(None, None, None, "azim", None),
        P(None, None, None, None, "azim", "axial"),
        P(None, "azim", "axial"),
        P(),
    )
    out_specs = P(None, None, None, None, "azim", "axial", None)
    return jax.shard_map(
        per_device, mesh=mesh, in_specs=in_specs, out_specs=out_specs, check_vma=False
    )
```
